128 devices in a mesh: orb: 32 (over y, x, core), fit: 4 (over z).
Axes of the slice: x: 4, y: 4, z: 4, core: 2. Of those that a mesh axis runs over, the one named last changes fastest.
Arguments:
- blocks: bfloat16 [128, 512, 2048], P('orb', None, 'fit'), may hold values from -1 to 1
- occ_energy: float32 [128], replicated, may hold values from -1.2 to -0.3
- virt_energy: float32 [128, 512], replicated, may hold values from 0.2 to 4
- domains: int32 [128], replicated, may hold values from 128 to 512, as said below
- pairs: int32 [512, 2], P('orb'), may hold values from 0 to 127, as said below
Outputs:
- gamma: float32 [128, 512, 2048], P('orb', None, 'fit')
- density: float32 [128, 512, 512], P('orb', None, 'fit')
The draws below stay inside these ranges and needn't reach their ends.
Inputs may be any that keep to these rules, and one draw needn't show every extreme that they name: `domains`: multiples of 128; some orbital has domain 512 and some has 128. Rows d * 16 to (d + 1) * 16 - 1 are the pairs of the d-th index of orb: their i lies in d * 4 to (d + 1) * 4 - 1. Within them, rows 2g and 2g + 1 have the same j and different i, and the 8 values j // 4 of these groups are all different. One index of orb is among these values for every index of orb.
All inputs are finite; a program needn't handle non-finite values.
Results may differ from the reference program's by a relative error of at most 0.02.
Values may be sent and summed in bfloat16 or wider, within the bound.
No kernel may reach another device: no remote copies, remote signals or barrier semaphores. Data moves between devices by JAX's collectives and lax.ppermute only.
A program may use at most 192 MiB of HBM per device.

```python
import math
import jax
import jax.numpy as jnp
from jax import lax

V = 512
NAUX = 2048
ORB_DEV = 4
FIT_BLOCKS = 4
NOCC = 128
PAIR_DEV = 16
PARTNERS = 8
NPAIRS = 512
N_ORB = 32


def draw_domains(key, part):
    key = jax.random.fold_in(key, 11)
    key_levels, key_spot = jax.random.split(key)
    levels = jax.random.randint(key_levels, (NOCC,), 1, 5) * (V // 4)
    spot = jax.random.randint(key_spot, (), 0, NOCC)
    levels = levels.at[spot].set(V)
    levels = levels.at[(spot + 1) % NOCC].set(V // 4)
    return levels.astype(jnp.int32)


def draw_pairs(key, part):
    key = jax.random.fold_in(key, 23)
    key_busy, key_rest = jax.random.split(key)
    busiest = jax.random.randint(key_busy, (), 0, N_ORB)

    def device_rows(device):
        device_key = jax.random.fold_in(key_rest, device)
        key_perm, key_first, key_step, key_right = jax.random.split(device_key, 4)
        owners = jax.random.permutation(key_perm, N_ORB)[:PARTNERS]
        present = jnp.any(owners == busiest)
        owners = jnp.where(present, owners, owners.at[0].set(busiest))
        first_local = jax.random.randint(key_first, (PARTNERS,), 0, ORB_DEV)
        second_local = (first_local + jax.random.randint(key_step, (PARTNERS,), 1, ORB_DEV)) % ORB_DEV
        left = device * ORB_DEV + jnp.stack([first_local, second_local], axis=1)
        right = owners * ORB_DEV + jax.random.randint(key_right, (PARTNERS,), 0, ORB_DEV)
        right = jnp.broadcast_to(right[:, None], (PARTNERS, 2))
        return jnp.stack([left, right], axis=2).reshape(PAIR_DEV, 2)
    rows = jax.vmap(device_rows)(jnp.arange(N_ORB))
    return rows.reshape(NPAIRS, 2).astype(jnp.int32)


def shard_levels(own_key, extent, shards, low, largest):
    def one(position, shards_of):
        steps = jax.random.uniform(jax.random.fold_in(jax.random.fold_in(own_key, 6), position), (shards_of,), jnp.float32, low / len(shards), largest / len(shards))
        return jnp.repeat(jnp.exp(steps), extent[position] // shards_of).reshape((-1,) + (1,) * (len(extent) - position - 1))

    gain = one(*shards[0])
    for cut in shards[1:]:
        gain = gain * one(*cut)
    return gain


def gaussian(key, extent, scale, reach, pieces=(), held_as=jnp.bfloat16):
    entries = jax.random.normal(key, extent, jnp.float32) * scale
    if len(pieces) > 0:
        entries = shard_levels(key, extent, pieces, -0.22, 0.18) * entries
    return jnp.clip(entries, min=-reach, max=reach).astype(held_as)


def setup_inputs(seed: int = 0) -> dict:
    key_list = jax.random.split(jax.random.key(seed), 6)
    blocks = gaussian(key_list[0], (NOCC, V, NAUX), 0.15, 1.0, ((0, 32), (2, 4)))
    occ_energy = jnp.clip(jax.random.uniform(key_list[1], (NOCC,), jnp.float32, -1.2, -0.3), -1.2, -0.3)
    virt_energy = jnp.clip(jnp.exp(jax.random.uniform(key_list[2], (NOCC, V), jnp.float32, math.log(0.2), math.log(4.0))), 0.2, 4.0)
    domains = draw_domains(jax.random.fold_in(key_list[5], 71), 0)
    pairs = draw_pairs(jax.random.fold_in(key_list[5], 71), 0)
    return dict(blocks=blocks, occ_energy=occ_energy, virt_energy=virt_energy, domains=domains, pairs=pairs)


def pair_terms(left, right, energy_left, energy_right, occ_left, occ_right, dom_left, dom_right):
    span = NAUX // FIT_BLOCKS
    integrals = jnp.zeros((V, V), jnp.float32)
    for block_index in range(FIT_BLOCKS):
        left_part = left[:, block_index * span:(block_index + 1) * span]
        right_part = right[:, block_index * span:(block_index + 1) * span]
        partial_value = jnp.dot(left_part, right_part.T, preferred_element_type=jnp.float32).astype(jnp.bfloat16)
        partial_value = lax.optimization_barrier(partial_value)
        integrals = integrals + partial_value.astype(jnp.float32)
    positions = jnp.arange(V, dtype=jnp.int32)
    keep = (positions[:, None] < dom_left) & (positions[None, :] < dom_right)
    denominators = energy_left[:, None] + energy_right[None, :] - occ_left - occ_right
    amplitudes = jnp.where(keep, -integrals / denominators, jnp.zeros((), jnp.float32)).astype(jnp.bfloat16)
    return amplitudes


def reference(blocks, occ_energy, virt_energy, domains, pairs):
    def visit(carry, group):
        gamma, density = carry
        second_orb = group[0, 1]
        right = blocks[second_orb]
        back_total = jnp.zeros((V, NAUX), jnp.float32)
        for member in range(2):
            first_orb = group[member, 0]
            left = blocks[first_orb]
            amplitudes = pair_terms(left, right, virt_energy[first_orb], virt_energy[second_orb],
                                    occ_energy[first_orb], occ_energy[second_orb],
                                    domains[first_orb], domains[second_orb])
            own_terms = jnp.dot(amplitudes, right, preferred_element_type=jnp.float32)
            back_total = back_total + jnp.dot(amplitudes.T, left, preferred_element_type=jnp.float32)
            gamma = gamma.at[first_orb].add(own_terms)
            density = density.at[first_orb].add(jnp.dot(amplitudes, amplitudes.T, preferred_element_type=jnp.float32))
        returned = back_total.astype(jnp.bfloat16)
        gamma = gamma.at[second_orb].add(returned.astype(jnp.float32))
        return (gamma, density), None

    start = (jnp.zeros((NOCC, V, NAUX), jnp.float32), jnp.zeros((NOCC, V, V), jnp.float32))
    groups = pairs.reshape(NPAIRS // 2, 2, 2)
    (gamma, density), unused = lax.scan(visit, start, groups)
    return gamma, density
```

```python
import jax
import jax.numpy as jnp
from jax import lax
from jax.experimental import pallas as pl
from jax.experimental.pallas import tpu as pltpu
from jax.sharding import PartitionSpec as P

TILE = 128
SUB = 16
CHUNKS = 2
F32 = jnp.float32
BF16 = jnp.bfloat16
VMEM_LIMIT = 56 * 1024 * 1024


def call(kernel, out_shape, args, *, scalars=0, scratch=(), flops=0, name=None):
    outs = out_shape if isinstance(out_shape, (tuple, list)) else (out_shape,)
    moved = sum(a.size * a.dtype.itemsize for a in args) + sum(
        o.size * jnp.dtype(o.dtype).itemsize for o in outs
    )
    in_specs = [pl.BlockSpec(memory_space=pltpu.SMEM)] * scalars + [
        pl.BlockSpec(memory_space=pltpu.VMEM)
    ] * (len(args) - scalars)
    specs = [pl.BlockSpec(memory_space=pltpu.VMEM)] * len(outs)
    return pl.pallas_call(
        kernel,
        out_shape=out_shape,
        in_specs=in_specs,
        out_specs=specs if isinstance(out_shape, (tuple, list)) else specs[0],
        scratch_shapes=list(scratch),
        compiler_params=pltpu.CompilerParams(vmem_limit_bytes=VMEM_LIMIT),
        cost_estimate=pl.CostEstimate(flops=flops, bytes_accessed=moved, transcendentals=0),
        name=name,
    )(*args)


def sds(shape, dtype):
    return jax.ShapeDtypeStruct(shape, dtype)


def pack_blocks(blocks, info, peers):
    orbs, virt, aux = blocks.shape
    tiles, cols = virt // TILE, aux // 128

    def kernel(blocks_ref, info_ref, out_ref):
        for m in range(peers):
            r, c = divmod(m, cols)
            for k in range(orbs):
                for t in range(tiles):
                    out_ref[m, k * tiles + t] = blocks_ref[
                        k, t * TILE + r * SUB : t * TILE + (r + 1) * SUB, c * 128 : (c + 1) * 128
                    ]
            out_ref[m, orbs * tiles] = info_ref[...]

    return call(kernel, sds((peers, orbs * tiles + 1, SUB, 128), BF16), (blocks, info), name="pack_blocks")


def pick_pieces(wanted, held, first, count, tiles, orbs):
    peers = held.shape[0]

    def kernel(wanted_ref, held_ref, out_ref):
        @pl.loop(0, peers)
        def _(d):
            for g in range(count):
                j = wanted_ref[d, first + g]
                out_ref[d, g * tiles : (g + 1) * tiles] = held_ref[
                    j // orbs, pl.ds((j % orbs) * tiles, tiles)
                ]

    return call(
        kernel, sds((peers, count * tiles, SUB, 128), BF16), (wanted, held), scalars=1, name="pick_pieces"
    )


def assemble_right(right_ref, pieces_ref, g, tiles, cols):
    peers = pieces_ref.shape[0]
    for t in range(tiles):
        for m in range(peers):
            r, c = divmod(m, cols)
            right_ref[t * TILE + r * SUB : t * TILE + (r + 1) * SUB, c * 128 : (c + 1) * 128] = pieces_ref[
                m, g * tiles + t
            ]


def partial_integrals(where, pairs_at, slots, pieces, blocks, room, fits):
    orbs, virt, aux = blocks.shape
    tiles, cols = virt // TILE, aux // 128
    groups = pieces.shape[1] // tiles
    rows = TILE // fits
    half = rows // 2
    wide = 2 * TILE

    def kernel(where_ref, left_ref, slot_ref, pieces_ref, blocks_ref, own_ref, up_ref, down_ref, up0_ref, down1_ref, right_ref, part_ref):
        f = where_ref[0]
        at = [pl.multiple_of(((f + k) % fits) * rows, rows) for k in range(fits)]

        @pl.loop(0, groups)
        def _(g):
            assemble_right(right_ref, pieces_ref, g, tiles, cols)
            for u in range(2):
                p = 2 * g + u
                for h in reversed(range(virt // wide)):
                    left = blocks_ref[left_ref[p], h * wide : (h + 1) * wide, :]
                    part_ref[...] = lax.dot_general(
                        right_ref[...], left, (((1,), (1,)), ((), ())), preferred_element_type=F32
                    ).astype(BF16)
                    for tb in reversed(range(tiles)):
                        for v in reversed(range(2)):
                            s = slot_ref[p, tb * tiles + 2 * h + v]
                            lanes = slice(v * TILE, (v + 1) * TILE)

                            def piece(k, offset, size):
                                return part_ref[pl.ds(tb * TILE + at[k] + offset, size), lanes]

                            own_ref[s] = piece(0, 0, rows)
                            up_ref[s, 0:half] = piece(2, 0, half)
                            up_ref[s, half:rows] = piece(1, half, half)
                            down_ref[s, 0:half] = piece(3, 0, half)
                            down_ref[s, half:rows] = piece(2, half, half)
                            up0_ref[s] = piece(1, 0, half)
                            down1_ref[s] = piece(3, half, half)

    full, part = sds((room, rows, TILE), BF16), sds((room, half, TILE), BF16)
    return call(
        kernel,
        [full, full, full, part, part],
        (where, pairs_at, slots, pieces, blocks),
        scalars=3,
        scratch=[pltpu.VMEM((virt, aux), BF16), pltpu.VMEM((virt, wide), BF16)],
        flops=4 * groups * virt * virt * aux,
        name="partial_integrals",
    )


def merge_halves(up, up0, down, down1):
    half = up0.shape[1]

    def kernel(up_ref, up0_ref, down_ref, down1_ref, more_up_ref, more_down_ref):
        more_up_ref[...] = (up_ref[:, 0:half].astype(F32) + up0_ref[...].astype(F32)).astype(BF16)
        more_down_ref[...] = (down_ref[:, half:].astype(F32) + down1_ref[...].astype(F32)).astype(BF16)

    out = sds(up0.shape, BF16)
    return call(kernel, [out, out], (up, up0, down, down1), name="merge_halves")


def make_amplitudes(slots, pairs_at, own, up, down, more_up, more_down, right_level, left_level, groups):
    room, rows, _ = own.shape
    half = rows // 2
    pair_tiles = slots.shape[1]
    tiles = right_level.shape[0] // groups

    def kernel(slot_ref, left_ref, own_ref, up_ref, down_ref, mup_ref, mdown_ref, rl_ref, ll_ref, z0_ref, z1_ref):
        @pl.loop(0, groups)
        def _(g):
            for u in range(2):
                p = 2 * g + u
                k = left_ref[p]
                for tile in reversed(range(pair_tiles)):
                    tb, ta = divmod(tile, tiles)
                    s = slot_ref[p, tile]
                    level = rl_ref[g * tiles + tb] + ll_ref[k * tiles + ta]
                    low = own_ref[s, 0:half].astype(F32) + down_ref[s, 0:half].astype(F32) + mup_ref[s].astype(F32)
                    high = own_ref[s, half:].astype(F32) + up_ref[s, half:].astype(F32) + mdown_ref[s].astype(F32)
                    z0_ref[s] = (-low / level[0:half]).astype(BF16)
                    z1_ref[s] = (-high / level[half:]).astype(BF16)

    out = sds((room, half, TILE), BF16)
    return call(
        kernel,
        [out, out],
        (slots, pairs_at, own, up, down, more_up, more_down, right_level, left_level),
        scalars=2,
        name="make_amplitudes",
    )


def assemble_amplitudes(amp_ref, amps, slot_ref, keep_ref, p, at, tiles, half):
    for tb in range(tiles):
        for ta in range(tiles):
            tile = tb * tiles + ta
            s = slot_ref[p, tile]
            keep = keep_ref[p, tile] > 0
            for k, pair in enumerate(amps):
                for h, ref in enumerate(pair):
                    value = ref[s]
                    amp_ref[pl.ds(tb * TILE + at[k] + h * half, half), ta * TILE : (ta + 1) * TILE] = jnp.where(
                        keep, value, jnp.zeros_like(value)
                    )


def returned_blocks(where, pairs_at, slots, keep, amps, blocks, peers, fits):
    orbs, virt, aux = blocks.shape
    tiles, cols = virt // TILE, aux // 128
    groups = slots.shape[0] // 2
    rows = TILE // fits
    half = rows // 2
    wide = 256

    def kernel(where_ref, left_ref, slot_ref, keep_ref, *refs):
        parts = refs[: 2 * fits]
        blocks_ref, out_ref, amp0_ref, amp1_ref = refs[2 * fits :]
        f = where_ref[0]
        at = [pl.multiple_of(((f + k) % fits) * rows, rows) for k in range(fits)]
        amps = [parts[2 * k : 2 * k + 2] for k in range(fits)]

        @pl.loop(0, groups)
        def _(g):
            assemble_amplitudes(amp0_ref, amps, slot_ref, keep_ref, 2 * g, at, tiles, half)
            assemble_amplitudes(amp1_ref, amps, slot_ref, keep_ref, 2 * g + 1, at, tiles, half)
            k0, k1 = left_ref[2 * g], left_ref[2 * g + 1]
            for h in range(aux // wide):
                lanes = slice(h * wide, (h + 1) * wide)
                back = (
                    jnp.dot(amp0_ref[...], blocks_ref[k0, :, lanes], preferred_element_type=F32)
                    + jnp.dot(amp1_ref[...], blocks_ref[k1, :, lanes], preferred_element_type=F32)
                ).astype(BF16)
                for t in range(tiles):
                    for r in range(TILE // SUB):
                        for c in range(wide // 128):
                            out_ref[r * cols + h * (wide // 128) + c, g * tiles + t] = back[
                                t * TILE + r * SUB : t * TILE + (r + 1) * SUB, c * 128 : (c + 1) * 128
                            ]

    return call(
        kernel,
        sds((peers, groups * tiles, SUB, 128), BF16),
        (where, pairs_at, slots, keep, *amps, blocks),
        scalars=4,
        scratch=[pltpu.VMEM((virt, virt), BF16)] * 2,
        flops=4 * groups * virt * virt * aux,
        name="returned_blocks",
    )


def own_terms(where, pairs_at, slots, keep, amps, pieces, orbs, virt, aux, fits):
    tiles, cols = virt // TILE, aux // 128
    chunks = len(pieces)
    groups = pieces[0].shape[1] // tiles
    rows = TILE // fits
    half = rows // 2

    def kernel(where_ref, left_ref, *refs):
        slot_refs, keep_refs = refs[:chunks], refs[chunks : 2 * chunks]
        refs = refs[2 * chunks :]
        amp_refs = refs[: 2 * fits * chunks]
        refs = refs[2 * fits * chunks :]
        piece_refs = refs[:chunks]
        gamma_ref, dens_ref, right_ref, amp_ref, turned_ref = refs[chunks:]
        f = where_ref[0]
        at = [pl.multiple_of(((f + k) % fits) * rows, rows) for k in range(fits)]
        mine = pl.ds(pl.multiple_of(f * (virt // fits), virt // fits), virt // fits)
        gamma_ref[...] = jnp.zeros_like(gamma_ref)
        dens_ref[...] = jnp.zeros_like(dens_ref)
        for n in range(chunks):
            flat = amp_refs[2 * fits * n : 2 * fits * (n + 1)]
            parts = [flat[2 * k : 2 * k + 2] for k in range(fits)]

            @pl.loop(0, groups)
            def _(g):
                assemble_right(right_ref, piece_refs[n], g, tiles, cols)
                for u in range(2):
                    p = 2 * g + u
                    k = left_ref[2 * groups * n + p]
                    assemble_amplitudes(amp_ref, parts, slot_refs[n], keep_refs[n], p, at, tiles, half)
                    turned_ref[...] = amp_ref[...].T
                    for h in range(2):
                        lanes = slice(h * (aux // 2), (h + 1) * (aux // 2))
                        gamma_ref[k, :, lanes] += jnp.dot(
                            turned_ref[...], right_ref[:, lanes], preferred_element_type=F32
                        )
                    dens_ref[k] += lax.dot_general(
                        turned_ref[...], turned_ref[mine, :], (((1,), (1,)), ((), ())), preferred_element_type=F32
                    )

    return call(
        kernel,
        [sds((orbs, virt, aux), F32), sds((orbs, virt, virt // fits), F32)],
        (where, pairs_at, *slots, *keep, *[a for part in amps for a in part], *pieces),
        scalars=2 + 2 * chunks,
        scratch=[pltpu.VMEM((virt, aux), BF16), pltpu.VMEM((virt, virt), BF16), pltpu.VMEM((virt, virt), BF16)],
        flops=5 * chunks * groups * virt * virt * aux,
        name="own_terms",
    )


def sum_returned(wanted, returned, orbs, tiles):
    peers = wanted.shape[0]
    count = returned[0].shape[1] // tiles

    def kernel(wanted_ref, *refs):
        parts, out_ref, total_ref = refs[: len(returned)], refs[-2], refs[-1]
        total_ref[...] = jnp.zeros_like(total_ref)
        for n, ref in enumerate(parts):

            @pl.loop(0, peers)
            def _(d):
                for g in range(count):
                    j = wanted_ref[d, n * count + g]
                    spot = pl.ds((j % orbs) * tiles, tiles)
                    total_ref[j // orbs, spot] += ref[d, g * tiles : (g + 1) * tiles].astype(F32)

        out_ref[...] = total_ref[...].astype(BF16)

    shape = (peers, orbs * tiles, SUB, 128)
    return call(
        kernel, sds(shape, BF16), (wanted, *returned), scalars=1, scratch=[pltpu.VMEM(shape, F32)], name="sum_returned"
    )


def add_returned(gamma_own, sums):
    orbs, virt, aux = gamma_own.shape
    tiles, cols = virt // TILE, aux // 128
    peers = sums.shape[0]

    def kernel(own_ref, sums_ref, out_ref):
        for t in range(tiles):
            for m in range(peers):
                r, c = divmod(m, cols)
                rows = slice(t * TILE + r * SUB, t * TILE + (r + 1) * SUB)
                lanes = slice(c * 128, (c + 1) * 128)
                out_ref[0, rows, lanes] = own_ref[0, rows, lanes] + sums_ref[m, t].astype(F32)

    return pl.pallas_call(
        kernel,
        grid=(orbs,),
        out_shape=sds((orbs, virt, aux), F32),
        in_specs=[
            pl.BlockSpec((1, virt, aux), lambda k: (k, 0, 0)),
            pl.BlockSpec((peers, tiles, SUB, 128), lambda k: (0, k, 0, 0)),
        ],
        out_specs=pl.BlockSpec((1, virt, aux), lambda k: (k, 0, 0)),
        compiler_params=pltpu.CompilerParams(vmem_limit_bytes=VMEM_LIMIT),
        cost_estimate=pl.CostEstimate(flops=0, bytes_accessed=10 * orbs * virt * aux, transcendentals=0),
        name="add_returned",
    )(gamma_own, sums)


def on_device(blocks, occ_energy, virt_energy, domains, pairs):
    peers = lax.axis_size("orb")
    fits = lax.axis_size("fit")
    my_index = lax.axis_index("orb")
    f = lax.axis_index("fit")
    orbs, virt, aux = blocks.shape
    tiles = virt // TILE
    pair_count = pairs.shape[0]
    group_count = pair_count // 2
    per = group_count // CHUNKS
    rows = TILE // fits

    left_orb = pairs[:, 0]
    pairs_at = (left_orb - my_index * orbs).astype(jnp.int32)
    right_orb = pairs[::2, 1]
    where = f.astype(jnp.int32).reshape(1)

    info = jnp.zeros((SUB, 128), BF16).at[0, :group_count].set(right_orb.astype(BF16))
    held = lax.all_to_all(pack_blocks(blocks, info, peers), "orb", split_axis=0, concat_axis=0, tiled=True)
    wanted = held[:, orbs * tiles, 0, :group_count].astype(jnp.int32)

    right_rows = jnp.take(virt_energy, right_orb, axis=0) - jnp.take(occ_energy, right_orb)[:, None]
    right_rows = lax.dynamic_slice_in_dim(right_rows.reshape(group_count * tiles, TILE), f * rows, rows, axis=1)
    right_level = jnp.broadcast_to(right_rows[:, :, None], (group_count * tiles, rows, TILE))
    my_orbs = my_index * orbs + jnp.arange(orbs, dtype=jnp.int32)
    left_rows = jnp.take(virt_energy, my_orbs, axis=0) - jnp.take(occ_energy, my_orbs)[:, None]
    left_level = left_rows.reshape(orbs * tiles, 1, TILE)

    span_left = jnp.take(domains, left_orb) // TILE
    span_right = jnp.take(domains, jnp.repeat(right_orb, 2)) // TILE
    tile_ids = jnp.arange(tiles, dtype=jnp.int32)
    keep = (
        (tile_ids[None, :, None] < span_right[:, None, None]) & (tile_ids[None, None, :] < span_left[:, None, None])
    ).astype(jnp.int32).reshape(pair_count, tiles * tiles)
    chunk_pairs = 2 * per
    room = chunk_pairs * tiles * tiles
    slots = jnp.arange(room, dtype=jnp.int32).reshape(chunk_pairs, tiles * tiles)

    up = [(k, (k + 1) % fits) for k in range(fits)]
    down = [(k, (k - 1) % fits) for k in range(fits)]

    pieces = [
        lax.all_to_all(
            pick_pieces(wanted, held, n * per, per, tiles, orbs), "orb", split_axis=0, concat_axis=0, tiled=True
        )
        for n in range(CHUNKS)
    ]
    all_amps, keeps, returned = [], [], []
    for n in range(CHUNKS):
        at = pairs_at[n * chunk_pairs : (n + 1) * chunk_pairs]
        kept = keep[n * chunk_pairs : (n + 1) * chunk_pairs]
        own, go_up, go_down, up0, down1 = partial_integrals(where, at, slots, pieces[n], blocks, room, fits)
        came_up = lax.ppermute(go_up, "fit", up)
        came_down = lax.ppermute(go_down, "fit", down)
        more_up, more_down = merge_halves(came_up, up0, came_down, down1)
        more_up = lax.ppermute(more_up, "fit", up)
        more_down = lax.ppermute(more_down, "fit", down)
        z0, z1 = make_amplitudes(
            slots, at, own, came_up, came_down, more_up, more_down,
            right_level[n * per * tiles : (n + 1) * per * tiles], left_level, per,
        )
        below0 = lax.ppermute(z0, "fit", up)
        above1 = lax.ppermute(z1, "fit", down)
        below1 = lax.ppermute(z1, "fit", up)
        above0 = lax.ppermute(z0, "fit", down)
        across0 = lax.ppermute(below0, "fit", up)
        across1 = lax.ppermute(above1, "fit", down)
        amps = [z0, z1, above0, above1, across0, across1, below0, below1]
        back = returned_blocks(where, at, slots, kept, amps, blocks, peers, fits)
        returned.append(lax.all_to_all(back, "orb", split_axis=0, concat_axis=0, tiled=True))
        all_amps.append(amps)
        keeps.append(kept)
    gamma_own, density = own_terms(
        where, pairs_at, [slots] * CHUNKS, keeps, all_amps, pieces, orbs, virt, aux, fits
    )
    sums = sum_returned(wanted, returned, orbs, tiles)
    sums = lax.all_to_all(sums, "orb", split_axis=0, concat_axis=0, tiled=True)
    return add_returned(gamma_own, sums), density


def solution(mesh):
    placed = (P("orb", None, "fit"), P(), P(), P(), P("orb", None))
    return jax.shard_map(
        on_device,
        mesh=mesh,
        in_specs=placed,
        out_specs=(P("orb", None, "fit"), P("orb", None, "fit")),
        check_vma=False,
    )
```

```python
import jax
import jax.numpy as jnp
from jax import lax
from jax.experimental import pallas as pl
from jax.experimental.pallas import tpu as pltpu
from jax.sharding import PartitionSpec as P

TILE = 128
SUB = 16
WIDE = 256
F32 = jnp.float32
BF16 = jnp.bfloat16
MIB = 1024 * 1024


ORB, FIT, BACK, MINE, NEXT = 0, 1, 2, 6, 10

SMEM = pl.BlockSpec(memory_space=pltpu.SMEM)
ANY = pl.BlockSpec(memory_space=pl.ANY)


def sds(shape, dtype):
    return jax.ShapeDtypeStruct(shape, dtype)


def whole(shape):
    return pl.BlockSpec(shape, lambda n: (0,) * len(shape))


def call(kernel, grid, in_specs, out_specs, out_shape, args, scratch=(), memory=56, name=None):
    return pl.pallas_call(
        kernel,
        grid=(grid,),
        in_specs=in_specs,
        out_specs=out_specs,
        out_shape=out_shape,
        scratch_shapes=list(scratch),
        compiler_params=pltpu.CompilerParams(vmem_limit_bytes=memory * MIB),
        cost_estimate=pl.CostEstimate(flops=0, bytes_accessed=1024, transcendentals=0),
        name=name,
    )(*args)


def device_of(m, fits, cols):
    return m // (fits * cols), m // cols % fits, m % cols


def pack_blocks(place, info, blocks, peers, fits):
    orbs, virt, aux = blocks.shape
    cols = aux // 128
    rows = TILE // fits

    def kernel(place_ref, info_ref, blocks_ref, out_ref):
        @pl.when(pl.program_id(0) < orbs)
        def _():
            for m in range(peers):
                h, turned, c = device_of(m, fits, cols)
                tile = place_ref[BACK + turned] * TILE
                for z in range(fits):
                    at = pl.multiple_of(tile + z * rows + h * SUB, SUB)
                    out_ref[m * fits + z, 0] = blocks_ref[0, pl.ds(at, SUB), c * 128 : (c + 1) * 128]

        @pl.when(pl.program_id(0) == orbs)
        def _():
            for m in range(peers * fits):
                out_ref[m, 0] = info_ref[...]

    return call(
        kernel,
        orbs + 1,
        [SMEM, whole(info.shape), pl.BlockSpec((1, virt, aux), lambda k: (jnp.minimum(k, orbs - 1), 0, 0))],
        pl.BlockSpec((peers * fits, 1, SUB, 128), lambda k: (0, k, 0, 0)),
        sds((peers * fits, orbs + 1, SUB, 128), BF16),
        (place, info, blocks),
        name="pack_blocks",
    )


def pick_pieces(place, wanted, held, fits, after):
    peers, count = wanted.shape
    orbs = held.shape[1] - 1
    block = peers // 4

    def kernel(place_ref, wanted_ref, held_ref, *refs):
        out_ref = refs[-1]
        parts = [place_ref[NEXT + s] for s in range(fits)]
        first = pl.program_id(0) * block

        @pl.loop(0, block)
        def _(d):
            for g in range(count):
                j = wanted_ref[first + d, g]
                source, k = lax.div(j, orbs) * fits, lax.rem(j, orbs)
                for s in range(fits):
                    out_ref[d, g * fits + s] = held_ref[source + parts[s], k]

    return call(
        kernel,
        4,
        [SMEM, SMEM, whole(held.shape)] + [ANY] * len(after),
        pl.BlockSpec((block, count * fits, SUB, 128), lambda n: (n, 0, 0, 0)),
        sds((peers, count * fits, SUB, 128), BF16),
        (place, wanted, held, *after),
        name="pick_pieces",
    )


def pair_terms(place, plan, left_levels, right_levels, pieces, lefts, fits):
    orbs, virt, aux = lefts[0].shape
    peers, count = pieces.shape[0], pieces.shape[1] // fits
    tiles, cols = virt // TILE, aux // 128
    rows = TILE // fits
    taken = tiles * rows
    wide = virt // fits
    half = orbs // 2
    names = ("left", "nleft", "nright")

    def kernel(place_ref, left_ref, nleft_ref, nright_ref, low_ref, high_ref, pieces_ref, *refs):
        sources, refs = refs[: len(lefts)], refs[len(lefts) :]
        out_ref, own_ref, *parts = refs[: 2 * fits]
        lefts_ref, rows_ref, turned_ref, amp_ref, all_ref, square_ref, sems = refs[2 * fits :]
        n = pl.program_id(0)
        targets = [lefts_ref.at[0]]
        for s in range(1, fits):
            targets += [lefts_ref.at[s, 0:half], lefts_ref.at[s, half:orbs]]
        copies = [pltpu.make_async_copy(a, b, sems.at[k]) for k, (a, b) in enumerate(zip(sources, targets))]

        @pl.when(n == 0)
        def _():
            for copy in copies:
                copy.start()
            all_ref[...] = jnp.zeros_like(all_ref)

        @pl.when(n < count)
        def _():
            g = n
            for m in range(peers):
                h, turned, c = device_of(m, fits, cols)
                for s in range(fits):
                    at = pl.multiple_of(place_ref[BACK + (turned - s) % fits] * rows + h * SUB, SUB)
                    rows_ref[g, pl.ds(at, SUB), s * aux + c * 128 : s * aux + (c + 1) * 128] = pieces_ref[m, s]

            @pl.when(n == 0)
            def _():
                for copy in copies:
                    copy.wait()

            turned_ref[...] = rows_ref[g].T
            row_id = lax.broadcasted_iota(jnp.int32, (WIDE, taken), 0)
            col_id = lax.broadcasted_iota(jnp.int32, (WIDE, taken), 1)
            for u in range(2):
                p = 2 * g + u
                k = left_ref[p]
                for start in range(0, virt, WIDE):
                    at = slice(start, start + WIDE)
                    total = jnp.zeros((WIDE, taken), F32)
                    for s in range(fits):
                        total += (
                            jnp.dot(
                                lefts_ref[s, k, at, :],
                                turned_ref[s * aux : (s + 1) * aux, :],
                                preferred_element_type=F32,
                            )
                            .astype(BF16)
                            .astype(F32)
                        )
                    keep = (row_id < nleft_ref[p] * TILE - start) & (col_id < nright_ref[g] * rows)
                    amp = jnp.where(keep, -total / (low_ref[k, at, :] + high_ref[g]), 0.0).astype(BF16)
                    all_ref[k, at, pl.ds(pl.multiple_of(g * taken, taken), taken)] = amp
                    amp_ref[u, :, at] = amp.T
            k0, k1 = left_ref[2 * g], left_ref[2 * g + 1]
            for s in range(fits):
                for start in range(0, aux, WIDE):
                    lanes = slice(start, start + WIDE)
                    back = (
                        jnp.dot(amp_ref[0], lefts_ref[s, k0, :, lanes], preferred_element_type=F32)
                        + jnp.dot(amp_ref[1], lefts_ref[s, k1, :, lanes], preferred_element_type=F32)
                    ).astype(BF16)
                    for t in range(tiles):
                        turned = place_ref[NEXT + (s + t) % fits]
                        for h in range(rows // SUB):
                            for c in range(WIDE // 128):
                                out_ref[(h * fits + turned) * cols + start // 128 + c, t] = back[
                                    t * rows + h * SUB : t * rows + (h + 1) * SUB, c * 128 : (c + 1) * 128
                                ]

        for low in range(2):

            @pl.when((n >= count + low * half) & (n < count + (low + 1) * half))
            def _(low=low):
                k = n - count
                square_ref[...] = lax.dot_general(
                    all_ref[k], all_ref[k], (((1,), (1,)), ((), ())), preferred_element_type=F32
                ).astype(BF16)
                for s, target in enumerate([own_ref, *[parts[2 * s + low] for s in range(fits - 1)]]):
                    for start in range(0, aux, WIDE):
                        at = slice(s * aux + start, s * aux + start + WIDE)
                        right = rows_ref[:, :, at].reshape(count * taken, WIDE)
                        target[0, :, start : start + WIDE] = jnp.dot(
                            all_ref[k], right, preferred_element_type=F32
                        ).astype(BF16)
                    mine = pl.ds(pl.multiple_of(place_ref[NEXT + s] * wide, wide), wide)
                    target[0, :, aux : aux + wide] = square_ref[:, mine]

    block = (1, virt, aux + wide)
    places = [
        pl.BlockSpec(block, lambda n: (jnp.clip(n - count, 0, half - 1), 0, 0)),
        pl.BlockSpec(block, lambda n: (jnp.clip(n - count - half, 0, half - 1), 0, 0)),
    ]
    return call(
        kernel,
        count + orbs,
        [SMEM] * 4
        + [
            whole(left_levels.shape),
            whole(right_levels.shape),
            pl.BlockSpec((peers, fits, SUB, 128), lambda n: (0, jnp.minimum(n, count - 1), 0, 0)),
        ]
        + [ANY] * len(lefts),
        [
            pl.BlockSpec((peers, tiles, SUB, 128), lambda n: (0, jnp.minimum(n, count - 1), 0, 0)),
            pl.BlockSpec(block, lambda n: (jnp.maximum(n - count, 0), 0, 0)),
        ]
        + places * (fits - 1),
        [sds((peers, count * tiles, SUB, 128), BF16), sds((orbs, virt, aux + wide), BF16)]
        + [sds((half, virt, aux + wide), BF16)] * (2 * (fits - 1)),
        (place, *[plan[n] for n in names], left_levels, right_levels, pieces, *lefts),
        scratch=[
            pltpu.VMEM((fits, orbs, virt, aux), BF16),
            pltpu.VMEM((count, taken, fits * aux), BF16),
            pltpu.VMEM((fits * aux, taken), BF16),
            pltpu.VMEM((2, taken, virt), BF16),
            pltpu.VMEM((orbs, virt, count * taken), BF16),
            pltpu.VMEM((virt, virt), BF16),
            pltpu.SemaphoreType.DMA((len(lefts),)),
        ],
        name="pair_terms",
    )


def merge(mine, came, straight):
    half, virt, width = came[0].shape

    def kernel(a_ref, b_ref, c_ref, d_ref, e_ref, f_ref, up_ref, down_ref):
        n = pl.program_id(0)

        @pl.when(n < half)
        def _():
            up_ref[...] = (a_ref[...].astype(F32) + c_ref[...].astype(F32)).astype(BF16)
            down_ref[...] = f_ref[...]

        @pl.when(n >= half)
        def _():
            up_ref[...] = e_ref[...]
            down_ref[...] = (b_ref[...].astype(F32) + d_ref[...].astype(F32)).astype(BF16)

    block = (1, virt, width)
    first = pl.BlockSpec(block, lambda n: (jnp.minimum(n, half - 1), 0, 0))
    second = pl.BlockSpec(block, lambda n: (jnp.maximum(n - half, 0), 0, 0))
    every = pl.BlockSpec(block, lambda n: (n, 0, 0))
    return call(
        kernel,
        2 * half,
        [first, second, first, second, second, first],
        [every] * 2,
        [sds((2 * half, virt, width), BF16)] * 2,
        (*mine, *came, *straight),
        name="merge",
    )


def sum_returned(place, wanted, returned, orbs, fits, after):
    peers, count = wanted.shape
    tiles = fits
    steps = 4
    block = peers // steps

    def kernel(place_ref, wanted_ref, part_ref, *refs):
        out_ref, total_ref = refs[len(after) :]
        n = pl.program_id(0)

        @pl.when(n == 0)
        def _():
            total_ref[...] = jnp.zeros_like(total_ref)

        @pl.loop(0, block)
        def _(d):
            for g in range(count):
                spot = pl.ds(wanted_ref[n * block + d, g] * tiles, tiles)
                total_ref[spot] += part_ref[d, g * tiles : (g + 1) * tiles].astype(F32)

        @pl.when(n == steps - 1)
        def _():
            tile = [place_ref[MINE + q] for q in range(fits)]

            @pl.loop(0, peers)
            def _(o):
                for q in range(fits):
                    for k in range(orbs):
                        out_ref[o * fits + q, k] = total_ref[(o * orbs + k) * tiles + tile[q]].astype(BF16)

    out = (peers * fits, orbs, SUB, 128)
    return call(
        kernel,
        steps,
        [SMEM, SMEM, pl.BlockSpec((block, count * tiles, SUB, 128), lambda n: (n, 0, 0, 0))] + [ANY] * len(after),
        whole(out),
        sds(out, BF16),
        (place, wanted, returned, *after),
        scratch=[pltpu.VMEM((peers * orbs * tiles, SUB, 128), F32)],
        name="sum_returned",
    )


def add_all(place, own, below, above, sums, fits):
    orbs, virt, width = own.shape
    wide = virt // fits
    aux = width - wide
    cols = aux // 128
    rows = TILE // fits
    peers = sums.shape[0] // fits

    def kernel(place_ref, own_ref, below_ref, above_ref, sums_ref, gamma_ref, dens_ref):
        total = own_ref[0].astype(F32) + below_ref[0].astype(F32) + above_ref[0].astype(F32)
        gamma_ref[0] = total[:, 0:aux]
        dens_ref[0] = total[:, aux:width]
        for m in range(peers):
            h, turned, c = device_of(m, fits, cols)
            tile = place_ref[BACK + turned] * TILE
            lanes = slice(c * 128, (c + 1) * 128)
            for z in range(fits):
                at = pl.ds(pl.multiple_of(tile + z * rows + h * SUB, SUB), SUB)
                gamma_ref[0, at, lanes] += sums_ref[m * fits + z, 0].astype(F32)

    block = pl.BlockSpec((1, virt, width), lambda k: (k, 0, 0))
    return call(
        kernel,
        orbs,
        [SMEM, block, block, block, pl.BlockSpec((peers * fits, 1, SUB, 128), lambda k: (0, k, 0, 0))],
        [pl.BlockSpec((1, virt, aux), lambda k: (k, 0, 0)), pl.BlockSpec((1, virt, wide), lambda k: (k, 0, 0))],
        [sds((orbs, virt, aux), F32), sds((orbs, virt, wide), F32)],
        (place, own, below, above, sums),
        name="add_all",
    )


def on_device(blocks, occ_energy, virt_energy, domains, pairs):
    peers = lax.axis_size("orb")
    fits = lax.axis_size("fit")
    orbs, virt, aux = blocks.shape
    cols = aux // 128
    orb, fit = lax.axis_index("orb"), lax.axis_index("fit")
    steps = jnp.arange(fits, dtype=jnp.int32)
    place = jnp.concatenate(
        [jnp.stack([orb, fit]), (steps - fit) % fits, (orb // cols - steps) % fits, (fit + steps) % fits]
    ).astype(jnp.int32)

    def shift(x, k):
        return lax.ppermute(x, "fit", [(n, (n + k) % fits) for n in range(fits)])

    def to_orb(x):
        return lax.all_to_all(x, "orb", split_axis=0, concat_axis=0, tiled=True)

    def to_all(x):
        return lax.all_to_all(x, ("orb", "fit"), split_axis=0, concat_axis=0, tiled=True)

    low, high = blocks[: orbs // 2], blocks[orbs // 2 :]
    last0, next1 = shift(low, 1), shift(high, fits - 1)
    far0, far1 = shift(last0, 1), shift(next1, fits - 1)
    low, high, _, _ = lax.optimization_barrier((low, high, last0, next1))
    last1, next0 = shift(high, 1), shift(low, fits - 1)
    lefts = [blocks, next0, next1, far0, far1, last0, last1]
    right = pairs[::2, 1]
    groups = right.shape[0]
    info = jnp.zeros((SUB, 128), BF16).at[0, :groups].set(right.astype(BF16))
    held = to_all(pack_blocks(place, info, blocks, peers, fits))
    wanted = held[::fits, orbs, 0, :groups].astype(jnp.int32)
    spans = domains // TILE
    plan = dict(
        left=pairs[:, 0] - orb.astype(jnp.int32) * orbs,
        nleft=jnp.take(spans, pairs[:, 0]),
        nright=jnp.take(spans, right),
    )
    local = orb.astype(jnp.int32) * orbs + jnp.arange(orbs, dtype=jnp.int32)
    left_levels = (jnp.take(virt_energy, local, axis=0) - jnp.take(occ_energy, local)[:, None])[:, :, None]
    right_levels = jnp.take(virt_energy, right, axis=0) - jnp.take(occ_energy, right)[:, None]
    right_levels = lax.dynamic_slice_in_dim(
        right_levels.reshape(groups, -1, TILE), fit * (TILE // fits), TILE // fits, axis=2
    ).reshape(groups, 1, virt // fits)

    pieces = to_orb(pick_pieces(place, wanted, held, fits, after=[]))
    back, own, next0, next1, far0, far1, last0, last1 = pair_terms(
        place, plan, left_levels, right_levels, pieces, lefts, fits
    )
    returned = to_orb(back)
    far0, far1 = shift(far0, 1), shift(far1, fits - 1)
    rise, fall = merge((next0, last1), (far0, far1), (next1, last0))
    below, above = shift(rise, 1), shift(fall, fits - 1)
    total = to_all(sum_returned(place, wanted, returned, orbs, fits, after=[rise]))
    return tuple(add_all(place, own, below, above, total, fits))


def solution(mesh):
    placed = (P("orb", None, "fit"), P(), P(), P(), P("orb", None))
    return jax.shard_map(
        on_device,
        mesh=mesh,
        in_specs=placed,
        out_specs=(P("orb", None, "fit"), P("orb", None, "fit")),
        check_vma=False,
    )
```

```python
import jax
import jax.numpy as jnp
from jax import lax
from jax.experimental import pallas as pl
from jax.experimental.pallas import tpu as pltpu
from jax.sharding import PartitionSpec as P

TILE = 128
SUB = 16
WIDE = 256
DIGITS = ((2, 1), (4, 2), (4, 8))
F32 = jnp.float32
BF16 = jnp.bfloat16
MIB = 1024 * 1024


ORB, FIT, BACK, MINE, NEXT = 0, 1, 2, 6, 10

SMEM = pl.BlockSpec(memory_space=pltpu.SMEM)
ANY = pl.BlockSpec(memory_space=pl.ANY)


def sds(shape, dtype):
    return jax.ShapeDtypeStruct(shape, dtype)


def whole(shape):
    return pl.BlockSpec(shape, lambda n: (0,) * len(shape))


def call(kernel, grid, in_specs, out_specs, out_shape, args, scratch=(), memory=56, aliases=None, name=None):
    return pl.pallas_call(
        kernel,
        grid=(grid,),
        in_specs=in_specs,
        out_specs=out_specs,
        out_shape=out_shape,
        scratch_shapes=list(scratch),
        compiler_params=pltpu.CompilerParams(vmem_limit_bytes=memory * MIB),
        cost_estimate=pl.CostEstimate(flops=0, bytes_accessed=1024, transcendentals=0),
        input_output_aliases=aliases or {},
        name=name,
    )(*args)


def device_of(m, fits, cols):
    return m // (fits * cols), m // cols % fits, m % cols


def list_row(me, d):
    return sum(((me // stride - d // stride) & (count - 1)) * stride for count, stride in DIGITS)


def pack_blocks(place, blocks, peers, fits):
    orbs, virt, aux = blocks.shape
    cols = aux // 128
    rows = TILE // fits
    steps = 4
    block = peers // steps

    def kernel(place_ref, blocks_ref, out_ref):
        @pl.loop(0, block)
        def _(n):
            m = pl.program_id(0) * block + n
            h, turned, c = m // (fits * cols), m // cols % fits, m % cols
            tile = place_ref[BACK + turned] * TILE
            lanes = pl.ds(pl.multiple_of(c * 128, 128), 128)
            for z in range(fits):
                at = pl.ds(pl.multiple_of(tile + z * rows + h * SUB, SUB), SUB)
                for k in range(orbs):
                    out_ref[n * fits + z, k] = blocks_ref[k, at, lanes]

    return call(
        kernel,
        steps,
        [SMEM, whole(blocks.shape)],
        pl.BlockSpec((block * fits, orbs, SUB, 128), lambda n: (n, 0, 0, 0)),
        sds((peers * fits, orbs, SUB, 128), BF16),
        (place, blocks),
        name="pack_blocks",
    )


def pick_pieces(place, wanted, held, fits, after):
    peers, count = wanted.shape
    orbs = held.shape[1]
    block = peers // 4

    def kernel(place_ref, wanted_ref, held_ref, *refs):
        out_ref = refs[-1]
        parts = [place_ref[NEXT + s] for s in range(fits)]
        first = pl.program_id(0) * block

        @pl.loop(0, block)
        def _(d):
            row = list_row(place_ref[ORB], first + d)
            for g in range(count):
                j = wanted_ref[row, g]
                source, k = lax.div(j, orbs) * fits, lax.rem(j, orbs)
                for s in range(fits):
                    out_ref[d, g * fits + s] = held_ref[source + parts[s], k]

    return call(
        kernel,
        4,
        [SMEM, SMEM, whole(held.shape)] + [ANY] * len(after),
        pl.BlockSpec((block, count * fits, SUB, 128), lambda n: (n, 0, 0, 0)),
        sds((peers, count * fits, SUB, 128), BF16),
        (place, wanted, held, *after),
        name="pick_pieces",
    )


def pair_terms(place, plan, left_levels, right_levels, pieces, lefts, fits):
    orbs, virt, aux = lefts[0][0].shape
    peers, count = pieces.shape[0], pieces.shape[1] // fits
    tiles, cols = virt // TILE, aux // 128
    rows = TILE // fits
    taken = tiles * rows
    wide = virt // fits
    half = orbs // 2
    names = ("left", "nleft", "nright")

    def kernel(place_ref, left_ref, nleft_ref, nright_ref, low_ref, high_ref, pieces_ref, *refs):
        sources, refs = refs[: len(lefts)], refs[len(lefts) :]
        out_ref, all_out_ref, rows_out_ref, *far_refs = refs[:5]
        lefts_ref, rows_ref, turned_ref, amp_ref, all_ref, sems = refs[5:]
        n = pl.program_id(0)
        copies = [
            pltpu.make_async_copy(source, lefts_ref.at[s, first : first + array.shape[0]], sems.at[k])
            for k, (source, (array, s, first)) in enumerate(zip(sources, lefts))
        ]

        @pl.when(n == 0)
        def _():
            for copy in copies:
                copy.start()
            all_ref[...] = jnp.zeros_like(all_ref)

        @pl.when(n < count)
        def _():
            g = n
            for m in range(peers):
                h, turned, c = device_of(m, fits, cols)
                for s in range(fits):
                    at = pl.multiple_of(place_ref[BACK + (turned - s) % fits] * rows + h * SUB, SUB)
                    rows_ref[g, pl.ds(at, SUB), s * aux + c * 128 : s * aux + (c + 1) * 128] = pieces_ref[m, s]

            @pl.when(n == 0)
            def _():
                for copy in copies:
                    copy.wait()

            rows_out_ref[0] = rows_ref[g]
            turned_ref[...] = rows_ref[g].T
            row_id = lax.broadcasted_iota(jnp.int32, (WIDE, taken), 0)
            col_id = lax.broadcasted_iota(jnp.int32, (WIDE, taken), 1)
            for u in range(2):
                p = 2 * g + u
                k = left_ref[p]
                for start in range(0, virt, WIDE):
                    at = slice(start, start + WIDE)
                    total = jnp.zeros((WIDE, taken), F32)
                    for s in range(fits):
                        total += (
                            jnp.dot(
                                lefts_ref[s, k, at, :],
                                turned_ref[s * aux : (s + 1) * aux, :],
                                preferred_element_type=F32,
                            )
                            .astype(BF16)
                            .astype(F32)
                        )
                    keep = (row_id < nleft_ref[p] * TILE - start) & (col_id < nright_ref[g] * rows)
                    amp = jnp.where(keep, -total / (low_ref[k, at, :] + high_ref[g]), 0.0).astype(BF16)
                    all_ref[k, at, pl.ds(pl.multiple_of(g * taken, taken), taken)] = amp
                    amp_ref[u, :, at] = amp.T
            k0, k1 = left_ref[2 * g], left_ref[2 * g + 1]
            for s in range(fits):
                for start in range(0, aux, WIDE):
                    lanes = slice(start, start + WIDE)
                    back = (
                        jnp.dot(amp_ref[0], lefts_ref[s, k0, :, lanes], preferred_element_type=F32)
                        + jnp.dot(amp_ref[1], lefts_ref[s, k1, :, lanes], preferred_element_type=F32)
                    ).astype(BF16)
                    for t in range(tiles):
                        turned = place_ref[NEXT + (s + t) % fits]
                        for h in range(rows // SUB):
                            for c in range(WIDE // 128):
                                out_ref[(h * fits + turned) * cols + start // 128 + c, t] = back[
                                    t * rows + h * SUB : t * rows + (h + 1) * SUB, c * 128 : (c + 1) * 128
                                ]

        for low in range(2):

            @pl.when((n >= count + low * half) & (n < count + (low + 1) * half))
            def _(low=low):
                k = n - count
                all_out_ref[0] = all_ref[k]
                sum_part(place_ref, all_ref.at[k], rows_ref, fits // 2, far_refs[low])

    block = (1, virt, aux + wide)
    places = [
        pl.BlockSpec(block, lambda n: (jnp.clip(n - count, 0, half - 1), 0, 0)),
        pl.BlockSpec(block, lambda n: (jnp.clip(n - count - half, 0, half - 1), 0, 0)),
    ]
    return call(
        kernel,
        count + orbs,
        [SMEM] * 4
        + [
            whole(left_levels.shape),
            whole(right_levels.shape),
            pl.BlockSpec((peers, fits, SUB, 128), lambda n: (0, jnp.minimum(n, count - 1), 0, 0)),
        ]
        + [ANY] * len(lefts),
        [
            pl.BlockSpec((peers, tiles, SUB, 128), lambda n: (0, jnp.minimum(n, count - 1), 0, 0)),
        ]
        + [
            pl.BlockSpec((1, virt, count * taken), lambda n: (jnp.maximum(n - count, 0), 0, 0)),
            pl.BlockSpec((1, taken, fits * aux), lambda n: (jnp.minimum(n, count - 1), 0, 0)),
        ]
        + places,
        [
            sds((peers, count * tiles, SUB, 128), BF16),
            sds((orbs, virt, count * taken), BF16),
            sds((count, taken, fits * aux), BF16),
        ]
        + [sds((half, virt, aux + wide), BF16)] * 2,
        (place, *[plan[n] for n in names], left_levels, right_levels, pieces, *[array for array, _, _ in lefts]),
        scratch=[
            pltpu.VMEM((fits, orbs, virt, aux), BF16),
            pltpu.VMEM((count, taken, fits * aux), BF16),
            pltpu.VMEM((fits * aux, taken), BF16),
            pltpu.VMEM((2, taken, virt), BF16),
            pltpu.VMEM((orbs, virt, count * taken), BF16),
            pltpu.SemaphoreType.DMA((len(lefts),)),
        ],
        name="pair_terms",
    )


def sum_part(place_ref, all_ref, rows_ref, s, out_ref):
    virt, depth = all_ref.shape
    aux = out_ref.shape[2] * rows_ref.shape[2] // (rows_ref.shape[2] + virt)
    wide = out_ref.shape[2] - aux
    for start in range(0, aux, WIDE):
        right = rows_ref[:, :, s * aux + start : s * aux + start + WIDE].reshape(depth, WIDE)
        out_ref[0, :, start : start + WIDE] = jnp.dot(
            all_ref[...], right, preferred_element_type=F32
        ).astype(BF16)
    mine = pl.ds(pl.multiple_of(place_ref[NEXT + s] * wide, wide), wide)
    out_ref[0, :, aux : aux + wide] = lax.dot_general(
        all_ref[...], all_ref[mine, :], (((1,), (1,)), ((), ())), preferred_element_type=F32
    ).astype(BF16)


def near_terms(place, amps, rows, fits):
    orbs, virt, depth = amps.shape
    aux = rows.shape[2] // fits
    block = (1, virt, aux + virt // fits)

    def kernel(place_ref, all_ref, rows_ref, *out_refs):
        for s, out_ref in zip((0, 1, fits - 1), out_refs):
            sum_part(place_ref, all_ref.at[0], rows_ref, s, out_ref)

    return call(
        kernel,
        orbs,
        [SMEM, pl.BlockSpec((1, virt, depth), lambda k: (k, 0, 0)), whole(rows.shape)],
        [pl.BlockSpec(block, lambda k: (k, 0, 0))] * 3,
        [sds((orbs, *block[1:]), BF16)] * 3,
        (place, amps, rows),
        name="near_terms",
    )


def merge(rise, fall, far):
    orbs, virt, width = rise.shape
    half = orbs // 2

    def kernel(a_ref, b_ref, c_ref, d_ref, up_ref, down_ref):
        up_ref[...] = (a_ref[...].astype(F32) + c_ref[...].astype(F32)).astype(BF16)
        down_ref[...] = (b_ref[...].astype(F32) + d_ref[...].astype(F32)).astype(BF16)

    block = (1, virt, width)
    low = pl.BlockSpec(block, lambda n: (n, 0, 0))
    high = pl.BlockSpec(block, lambda n: (n + half, 0, 0))
    return call(
        kernel,
        half,
        [low, high, low, low],
        [low, high],
        [sds(rise.shape, BF16)] * 2,
        (rise, fall, *far),
        aliases={0: 0, 1: 1},
        name="merge",
    )


def sum_returned(place, wanted, returned, orbs, fits, after):
    peers, count = wanted.shape
    tiles = fits
    steps = 4
    block = peers // steps

    def kernel(place_ref, wanted_ref, part_ref, *refs):
        out_ref, total_ref = refs[len(after) :]
        n = pl.program_id(0)

        @pl.when(n == 0)
        def _():
            total_ref[...] = jnp.zeros_like(total_ref)

        @pl.loop(0, block)
        def _(d):
            row = list_row(place_ref[ORB], n * block + d)
            for g in range(count):
                spot = pl.ds(wanted_ref[row, g] * tiles, tiles)
                total_ref[spot] += part_ref[d, g * tiles : (g + 1) * tiles].astype(F32)

        @pl.when(n == steps - 1)
        def _():
            tile = [place_ref[MINE + q] for q in range(fits)]

            @pl.loop(0, peers)
            def _(o):
                for q in range(fits):
                    for k in range(orbs):
                        out_ref[o * fits + q, k] = total_ref[(o * orbs + k) * tiles + tile[q]].astype(BF16)

    out = (peers * fits, orbs, SUB, 128)
    return call(
        kernel,
        steps,
        [SMEM, SMEM, pl.BlockSpec((block, count * tiles, SUB, 128), lambda n: (n, 0, 0, 0))] + [ANY] * len(after),
        whole(out),
        sds(out, BF16),
        (place, wanted, returned, *after),
        scratch=[pltpu.VMEM((peers * orbs * tiles, SUB, 128), F32)],
        name="sum_returned",
    )


def add_all(place, own, below, above, sums, fits):
    orbs, virt, width = own.shape
    wide = virt // fits
    aux = width - wide
    cols = aux // 128
    rows = TILE // fits
    peers = sums.shape[0] // fits

    def kernel(place_ref, own_ref, below_ref, above_ref, sums_ref, gamma_ref, dens_ref):
        k = pl.program_id(0)
        total = own_ref[0].astype(F32) + below_ref[0].astype(F32) + above_ref[0].astype(F32)
        gamma_ref[0] = total[:, 0:aux]
        dens_ref[0] = total[:, aux:width]
        for m in range(peers):
            h, turned, c = device_of(m, fits, cols)
            tile = place_ref[BACK + turned] * TILE
            lanes = slice(c * 128, (c + 1) * 128)
            for z in range(fits):
                at = pl.ds(pl.multiple_of(tile + z * rows + h * SUB, SUB), SUB)
                gamma_ref[0, at, lanes] += sums_ref[m * fits + z, k].astype(F32)

    block = pl.BlockSpec((1, virt, width), lambda k: (k, 0, 0))
    return call(
        kernel,
        orbs,
        [SMEM, block, block, block, whole(sums.shape)],
        [pl.BlockSpec((1, virt, aux), lambda k: (k, 0, 0)), pl.BlockSpec((1, virt, wide), lambda k: (k, 0, 0))],
        [sds((orbs, virt, aux), F32), sds((orbs, virt, wide), F32)],
        (place, own, below, above, sums),
        name="add_all",
    )


def on_device(blocks, occ_energy, virt_energy, domains, pairs):
    peers = lax.axis_size("orb")
    fits = lax.axis_size("fit")
    orbs, virt, aux = blocks.shape
    cols = aux // 128
    orb, fit = lax.axis_index("orb"), lax.axis_index("fit")
    steps = jnp.arange(fits, dtype=jnp.int32)
    place = jnp.concatenate(
        [jnp.stack([orb, fit]), (steps - fit) % fits, (orb // cols - steps) % fits, (fit + steps) % fits]
    ).astype(jnp.int32)

    def shift(x, k):
        return lax.ppermute(x, "fit", [(n, (n + k) % fits) for n in range(fits)])

    def to_orb(x):
        return lax.all_to_all(x, "orb", split_axis=0, concat_axis=0, tiled=True)

    def to_all(x):
        return lax.all_to_all(x, ("orb", "fit"), split_axis=0, concat_axis=0, tiled=True)

    half = orbs // 2
    one = [blocks[k : k + 1] for k in range(orbs)]
    last0, next3 = shift(one[0], 1), shift(one[3], fits - 1)
    right = pairs[::2, 1]
    groups = right.shape[0]
    held = to_all(pack_blocks(place, blocks, peers, fits))
    wanted = jnp.pad(right[None], ((0, 0), (0, 128 - groups)))
    for count, stride in DIGITS:
        wanted = jnp.concatenate(
            [wanted]
            + [
                lax.ppermute(wanted, "orb", [(n, n + ((n // stride + k) % count - n // stride % count) * stride) for n in range(peers)])
                for k in range(1, count)
            ]
        )
    wanted = wanted[:, :groups]
    spans = domains // TILE
    plan = dict(
        left=pairs[:, 0] - orb.astype(jnp.int32) * orbs,
        nleft=jnp.take(spans, pairs[:, 0]),
        nright=jnp.take(spans, right),
    )
    local = orb.astype(jnp.int32) * orbs + jnp.arange(orbs, dtype=jnp.int32)
    left_levels = (jnp.take(virt_energy, local, axis=0) - jnp.take(occ_energy, local)[:, None])[:, :, None]
    right_levels = jnp.take(virt_energy, right, axis=0) - jnp.take(occ_energy, right)[:, None]
    right_levels = lax.dynamic_slice_in_dim(
        right_levels.reshape(groups, -1, TILE), fit * (TILE // fits), TILE // fits, axis=2
    ).reshape(groups, 1, virt // fits)

    pieces = to_orb(pick_pieces(place, wanted, held, fits, after=[last0, next3]))
    last1, next2 = shift(one[1], 1), shift(one[2], fits - 1)
    far0, far3 = shift(last0, 1), shift(next3, fits - 1)
    low, high, last1, next2 = lax.optimization_barrier((blocks[:half], blocks[half:], last1, next2))
    last2, next0 = shift(high, 1), shift(low, fits - 1)
    far1, far2 = shift(last1, 1), shift(next2, fits - 1)
    lefts = [(blocks, 0, 0), (next0, 1, 0), (next2, 1, 2), (next3, 1, 3)]
    lefts += [(last0, 3, 0), (last1, 3, 1), (last2, 3, 2)]
    lefts += [(far0, 2, 0), (far1, 2, 1), (far2, 2, 2), (far3, 2, 3)]
    back, amps, rows, *far = pair_terms(place, plan, left_levels, right_levels, pieces, lefts, fits)
    far = [shift(far[0], 1), shift(far[1], fits - 1)]
    returned = to_orb(back)
    own, rise, fall = near_terms(place, amps, rows, fits)
    rise, fall = merge(rise, fall, far)
    below, above = shift(rise, 1), shift(fall, fits - 1)
    total = to_all(sum_returned(place, wanted, returned, orbs, fits, after=[rise]))
    return tuple(add_all(place, own, below, above, total, fits))


def solution(mesh):
    placed = (P("orb", None, "fit"), P(), P(), P(), P("orb", None))
    return jax.shard_map(
        on_device,
        mesh=mesh,
        in_specs=placed,
        out_specs=(P("orb", None, "fit"), P("orb", None, "fit")),
        check_vma=False,
    )
```

```python
import jax
import jax.numpy as jnp
from jax import lax
from jax.experimental import pallas as pl
from jax.experimental.pallas import tpu as pltpu
from jax.sharding import PartitionSpec as P

TILE = 128
SUB = 16
WIDE = 256
DIGITS = ((2, 1), (4, 2), (4, 8))
F32 = jnp.float32
BF16 = jnp.bfloat16
MIB = 1024 * 1024


ORB, FIT, BACK, MINE, NEXT = 0, 1, 2, 6, 10

SMEM = pl.BlockSpec(memory_space=pltpu.SMEM)
ANY = pl.BlockSpec(memory_space=pl.ANY)


def sds(shape, dtype):
    return jax.ShapeDtypeStruct(shape, dtype)


def whole(shape):
    return pl.BlockSpec(shape, lambda n: (0,) * len(shape))


def call(kernel, grid, in_specs, out_specs, out_shape, args, scratch=(), memory=56, aliases=None, name=None):
    return pl.pallas_call(
        kernel,
        grid=(grid,),
        in_specs=in_specs,
        out_specs=out_specs,
        out_shape=out_shape,
        scratch_shapes=list(scratch),
        compiler_params=pltpu.CompilerParams(vmem_limit_bytes=memory * MIB),
        cost_estimate=pl.CostEstimate(flops=0, bytes_accessed=1024, transcendentals=0),
        input_output_aliases=aliases or {},
        name=name,
    )(*args)


def device_of(m, fits, cols):
    return m // (fits * cols), m // cols % fits, m % cols


def list_row(me, d):
    return sum(((me // stride - d // stride) & (count - 1)) * stride for count, stride in DIGITS)


def pack_blocks(place, blocks, peers, fits):
    orbs, virt, aux = blocks.shape
    cols = aux // 128
    rows = TILE // fits
    steps = 4
    block = peers // steps

    def kernel(place_ref, blocks_ref, out_ref):
        @pl.loop(0, block)
        def _(n):
            m = pl.program_id(0) * block + n
            h, turned, c = m // (fits * cols), m // cols % fits, m % cols
            tile = place_ref[BACK + turned] * TILE
            lanes = pl.ds(pl.multiple_of(c * 128, 128), 128)
            for z in range(fits):
                at = pl.ds(pl.multiple_of(tile + z * rows + h * SUB, SUB), SUB)
                for k in range(orbs):
                    out_ref[n * fits + z, k] = blocks_ref[k, at, lanes]

    return call(
        kernel,
        steps,
        [SMEM, whole(blocks.shape)],
        pl.BlockSpec((block * fits, orbs, SUB, 128), lambda n: (n, 0, 0, 0)),
        sds((peers * fits, orbs, SUB, 128), BF16),
        (place, blocks),
        name="pack_blocks",
    )


def pick_pieces(place, wanted, held, fits, after):
    peers, count = wanted.shape
    orbs = held.shape[1]
    held = held.reshape(-1, SUB, 128)
    block = peers // 4

    def kernel(place_ref, wanted_ref, held_ref, *refs):
        out_ref = refs[-1]
        parts = [place_ref[NEXT + s] * orbs for s in range(fits)]
        first = pl.program_id(0) * block

        @pl.loop(0, block)
        def _(d):
            row = list_row(place_ref[ORB], first + d)
            for g in range(count):
                spot = wanted_ref[row, g]
                for s in range(fits):
                    out_ref[d, g * fits + s] = held_ref[spot + parts[s]]

    return call(
        kernel,
        4,
        [SMEM, SMEM, whole(held.shape)] + [ANY] * len(after),
        pl.BlockSpec((block, count * fits, SUB, 128), lambda n: (n, 0, 0, 0)),
        sds((peers, count * fits, SUB, 128), BF16),
        (place, wanted, held, *after),
        name="pick_pieces",
    )


def pair_terms(place, plan, left_levels, right_levels, pieces, lefts, fits):
    orbs, virt, aux = lefts[0][0].shape
    peers, count = pieces.shape[0], pieces.shape[1] // fits
    tiles, cols = virt // TILE, aux // 128
    rows = TILE // fits
    taken = tiles * rows
    wide = virt // fits
    half = orbs // 2
    steps = count // 2
    names = ("left", "nleft", "nright")

    def kernel(place_ref, left_ref, nleft_ref, nright_ref, low_ref, high_ref, pieces_ref, *refs):
        sources, refs = refs[: len(lefts)], refs[len(lefts) :]
        out_ref, all_out_ref, rows_out_ref, *far_refs = refs[:5]
        lefts_ref, rows_ref, turned_ref, amp_ref, all_ref, sems = refs[5:]
        n = pl.program_id(0)
        copies = [
            pltpu.make_async_copy(source, lefts_ref.at[s, first : first + array.shape[0]], sems.at[k])
            for k, (source, (array, s, first)) in enumerate(zip(sources, lefts))
        ]

        @pl.when(n == 0)
        def _():
            for copy in copies:
                copy.start()
            all_ref[...] = jnp.zeros_like(all_ref)

        def group(g, e):
            for m in range(peers):
                h, turned, c = device_of(m, fits, cols)
                for s in range(fits):
                    at = pl.multiple_of(place_ref[BACK + (turned - s) % fits] * rows + h * SUB, SUB)
                    rows_out_ref[e, pl.ds(at, SUB), s * aux + c * 128 : s * aux + (c + 1) * 128] = pieces_ref[m, e * fits + s]

            if e == 0:

                @pl.when(n == 0)
                def _():
                    for copy in copies:
                        copy.wait()

            rows_ref[g] = rows_out_ref[e]
            turned_ref[e] = rows_out_ref[e].T
            row_id = lax.broadcasted_iota(jnp.int32, (WIDE, taken), 0)
            col_id = lax.broadcasted_iota(jnp.int32, (WIDE, taken), 1)
            for u in range(2):
                p = 2 * g + u
                k = left_ref[p]
                for start in range(0, virt, WIDE):
                    at = slice(start, start + WIDE)
                    total = jnp.zeros((WIDE, taken), F32)
                    for s in range(fits):
                        total += (
                            jnp.dot(
                                lefts_ref[s, k, at, :],
                                turned_ref[e, s * aux : (s + 1) * aux, :],
                                preferred_element_type=F32,
                            )
                            .astype(BF16)
                            .astype(F32)
                        )
                    keep = (row_id < nleft_ref[p] * TILE - start) & (col_id < nright_ref[g] * rows)
                    amp = jnp.where(keep, -total / (low_ref[k, at, :] + high_ref[g]), 0.0).astype(BF16)
                    all_ref[k, at, pl.ds(pl.multiple_of(g * taken, taken), taken)] = amp
                    amp_ref[e, u, :, at] = amp.T
            k0, k1 = left_ref[2 * g], left_ref[2 * g + 1]
            for s in range(fits):
                for start in range(0, aux, WIDE):
                    lanes = slice(start, start + WIDE)
                    back = (
                        jnp.dot(amp_ref[e, 0], lefts_ref[s, k0, :, lanes], preferred_element_type=F32)
                        + jnp.dot(amp_ref[e, 1], lefts_ref[s, k1, :, lanes], preferred_element_type=F32)
                    ).astype(BF16)
                    for t in range(tiles):
                        turned = place_ref[NEXT + (s + t) % fits]
                        for h in range(rows // SUB):
                            for c in range(WIDE // 128):
                                out_ref[(h * fits + turned) * cols + start // 128 + c, e * tiles + t] = back[
                                    t * rows + h * SUB : t * rows + (h + 1) * SUB, c * 128 : (c + 1) * 128
                                ]

        @pl.when(n < steps)
        def _():
            for e in range(2):
                group(2 * n + e, e)

        for low in range(2):

            @pl.when((n >= steps + low * half) & (n < steps + (low + 1) * half))
            def _(low=low):
                k = n - steps
                all_out_ref[0] = all_ref[k]
                sum_part(place_ref, all_ref.at[k], rows_ref, fits // 2, far_refs[low])

    block = (1, virt, aux + wide)
    places = [
        pl.BlockSpec(block, lambda n: (jnp.clip(n - steps, 0, half - 1), 0, 0)),
        pl.BlockSpec(block, lambda n: (jnp.clip(n - steps - half, 0, half - 1), 0, 0)),
    ]
    return call(
        kernel,
        steps + orbs,
        [SMEM] * 4
        + [
            whole(left_levels.shape),
            whole(right_levels.shape),
            pl.BlockSpec((peers, 2 * fits, SUB, 128), lambda n: (0, jnp.minimum(n, steps - 1), 0, 0)),
        ]
        + [ANY] * len(lefts),
        [
            pl.BlockSpec((peers, 2 * tiles, SUB, 128), lambda n: (0, jnp.minimum(n, steps - 1), 0, 0)),
        ]
        + [
            pl.BlockSpec((1, virt, count * taken), lambda n: (jnp.maximum(n - steps, 0), 0, 0)),
            pl.BlockSpec((2, taken, fits * aux), lambda n: (jnp.minimum(n, steps - 1), 0, 0)),
        ]
        + places,
        [
            sds((peers, count * tiles, SUB, 128), BF16),
            sds((orbs, virt, count * taken), BF16),
            sds((count, taken, fits * aux), BF16),
        ]
        + [sds((half, virt, aux + wide), BF16)] * 2,
        (place, *[plan[n] for n in names], left_levels, right_levels, pieces, *[array for array, _, _ in lefts]),
        scratch=[
            pltpu.VMEM((fits, orbs, virt, aux), BF16),
            pltpu.VMEM((count, taken, fits * aux), BF16),
            pltpu.VMEM((2, fits * aux, taken), BF16),
            pltpu.VMEM((2, 2, taken, virt), BF16),
            pltpu.VMEM((orbs, virt, count * taken), BF16),
            pltpu.SemaphoreType.DMA((len(lefts),)),
        ],
        name="pair_terms",
    )


def sum_part(place_ref, all_ref, rows_ref, s, out_ref):
    virt, depth = all_ref.shape
    aux = out_ref.shape[2] * rows_ref.shape[2] // (rows_ref.shape[2] + virt)
    wide = out_ref.shape[2] - aux
    for start in range(0, aux, WIDE):
        right = rows_ref[:, :, s * aux + start : s * aux + start + WIDE].reshape(depth, WIDE)
        out_ref[0, :, start : start + WIDE] = jnp.dot(
            all_ref[...], right, preferred_element_type=F32
        ).astype(BF16)
    mine = pl.ds(pl.multiple_of(place_ref[NEXT + s] * wide, wide), wide)
    out_ref[0, :, aux : aux + wide] = lax.dot_general(
        all_ref[...], all_ref[mine, :], (((1,), (1,)), ((), ())), preferred_element_type=F32
    ).astype(BF16)


def near_terms(place, amps, rows, fits):
    orbs, virt, depth = amps.shape
    aux = rows.shape[2] // fits
    block = (1, virt, aux + virt // fits)

    def kernel(place_ref, all_ref, rows_ref, *out_refs):
        for s, out_ref in zip((0, 1, fits - 1), out_refs):
            sum_part(place_ref, all_ref.at[0], rows_ref, s, out_ref)

    return call(
        kernel,
        orbs,
        [SMEM, pl.BlockSpec((1, virt, depth), lambda k: (k, 0, 0)), whole(rows.shape)],
        [pl.BlockSpec(block, lambda k: (k, 0, 0))] * 3,
        [sds((orbs, *block[1:]), BF16)] * 3,
        (place, amps, rows),
        name="near_terms",
    )


def merge(rise, fall, far):
    orbs, virt, width = rise.shape
    half = orbs // 2

    def kernel(a_ref, b_ref, c_ref, d_ref, up_ref, down_ref):
        up_ref[...] = (a_ref[...].astype(F32) + c_ref[...].astype(F32)).astype(BF16)
        down_ref[...] = (b_ref[...].astype(F32) + d_ref[...].astype(F32)).astype(BF16)

    block = (1, virt, width)
    low = pl.BlockSpec(block, lambda n: (n, 0, 0))
    high = pl.BlockSpec(block, lambda n: (n + half, 0, 0))
    return call(
        kernel,
        half,
        [low, high, low, low],
        [low, high],
        [sds(rise.shape, BF16)] * 2,
        (rise, fall, *far),
        aliases={0: 0, 1: 1},
        name="merge",
    )


def sum_returned(place, wanted, returned, orbs, fits, after):
    peers, count = wanted.shape
    tiles = fits
    steps = 4
    block = peers // steps

    def kernel(place_ref, wanted_ref, part_ref, *refs):
        out_ref, total_ref = refs[len(after) :]
        n = pl.program_id(0)

        @pl.when(n == 0)
        def _():
            total_ref[...] = jnp.zeros_like(total_ref)

        @pl.loop(0, block)
        def _(d):
            row = list_row(place_ref[ORB], n * block + d)
            for g in range(count):
                spot = wanted_ref[row, g]
                for t in range(tiles):
                    total_ref[spot + t * orbs] += part_ref[d, g * tiles + t].astype(F32)

        @pl.when(n == steps - 1)
        def _():
            tile = [place_ref[MINE + q] for q in range(fits)]

            @pl.loop(0, peers)
            def _(o):
                for q in range(fits):
                    out_ref[o * fits + q] = total_ref[pl.ds((o * tiles + tile[q]) * orbs, orbs)].astype(BF16)

    out = (peers * fits, orbs, SUB, 128)
    return call(
        kernel,
        steps,
        [SMEM, SMEM, pl.BlockSpec((block, count * tiles, SUB, 128), lambda n: (n, 0, 0, 0))] + [ANY] * len(after),
        whole(out),
        sds(out, BF16),
        (place, wanted, returned, *after),
        scratch=[pltpu.VMEM((peers * orbs * tiles, SUB, 128), F32)],
        name="sum_returned",
    )


def add_all(place, own, below, above, sums, fits):
    orbs, virt, width = own.shape
    wide = virt // fits
    aux = width - wide
    cols = aux // 128
    rows = TILE // fits
    peers = sums.shape[0] // fits

    def kernel(place_ref, own_ref, below_ref, above_ref, sums_ref, gamma_ref, dens_ref):
        total = own_ref[0].astype(F32) + below_ref[0].astype(F32) + above_ref[0].astype(F32)
        gamma_ref[0] = total[:, 0:aux]
        dens_ref[0] = total[:, aux:width]
        for m in range(peers):
            h, turned, c = device_of(m, fits, cols)
            tile = place_ref[BACK + turned] * TILE
            lanes = slice(c * 128, (c + 1) * 128)
            for z in range(fits):
                at = pl.ds(pl.multiple_of(tile + z * rows + h * SUB, SUB), SUB)
                gamma_ref[0, at, lanes] += sums_ref[m * fits + z, 0].astype(F32)

    block = pl.BlockSpec((1, virt, width), lambda k: (k, 0, 0))
    return call(
        kernel,
        orbs,
        [SMEM, block, block, block, pl.BlockSpec((peers * fits, 1, SUB, 128), lambda k: (0, k, 0, 0))],
        [pl.BlockSpec((1, virt, aux), lambda k: (k, 0, 0)), pl.BlockSpec((1, virt, wide), lambda k: (k, 0, 0))],
        [sds((orbs, virt, aux), F32), sds((orbs, virt, wide), F32)],
        (place, own, below, above, sums),
        name="add_all",
    )


def on_device(blocks, occ_energy, virt_energy, domains, pairs):
    peers = lax.axis_size("orb")
    fits = lax.axis_size("fit")
    orbs, virt, aux = blocks.shape
    cols = aux // 128
    orb, fit = lax.axis_index("orb"), lax.axis_index("fit")
    steps = jnp.arange(fits, dtype=jnp.int32)
    place = jnp.concatenate(
        [jnp.stack([orb, fit]), (steps - fit) % fits, (orb // cols - steps) % fits, (fit + steps) % fits]
    ).astype(jnp.int32)

    def shift(x, k):
        return lax.ppermute(x, "fit", [(n, (n + k) % fits) for n in range(fits)])

    def to_orb(x):
        return lax.all_to_all(x, "orb", split_axis=0, concat_axis=0, tiled=True)

    def to_all(x):
        return lax.all_to_all(x, ("orb", "fit"), split_axis=0, concat_axis=0, tiled=True)

    one = [blocks[k : k + 1] for k in range(orbs)]
    last0, next3 = shift(one[0], 1), shift(one[3], fits - 1)
    right = pairs[::2, 1]
    groups = right.shape[0]
    held = to_all(pack_blocks(place, blocks, peers, fits))
    wanted = jnp.pad((right // orbs * (fits * orbs) + right % orbs)[None], ((0, 0), (0, 128 - groups)))
    for count, stride in DIGITS:
        wanted = jnp.concatenate(
            [wanted]
            + [
                lax.ppermute(wanted, "orb", [(n, n + ((n // stride + k) % count - n // stride % count) * stride) for n in range(peers)])
                for k in range(1, count)
            ]
        )
    wanted = wanted[:, :groups]
    spans = domains // TILE
    plan = dict(
        left=pairs[:, 0] - orb.astype(jnp.int32) * orbs,
        nleft=jnp.take(spans, pairs[:, 0]),
        nright=jnp.take(spans, right),
    )
    local = orb.astype(jnp.int32) * orbs + jnp.arange(orbs, dtype=jnp.int32)
    left_levels = (jnp.take(virt_energy, local, axis=0) - jnp.take(occ_energy, local)[:, None])[:, :, None]
    right_levels = jnp.take(virt_energy, right, axis=0) - jnp.take(occ_energy, right)[:, None]
    right_levels = lax.dynamic_slice_in_dim(
        right_levels.reshape(groups, -1, TILE), fit * (TILE // fits), TILE // fits, axis=2
    ).reshape(groups, 1, virt // fits)

    pieces = to_orb(pick_pieces(place, wanted, held, fits, after=[last0, next3]))
    last, next_ = shift(blocks[1:], 1), shift(blocks[:-1], fits - 1)
    far0, far3 = shift(last0, 1), shift(next3, fits - 1)
    far1, far2 = shift(last[:1], 1), shift(next_[-1:], fits - 1)
    lefts = [(blocks, 0, 0), (next_, 1, 0), (next3, 1, orbs - 1), (last0, 3, 0), (last, 3, 1)]
    lefts += [(far0, 2, 0), (far1, 2, 1), (far2, 2, 2), (far3, 2, 3)]
    back, amps, rows, *far = pair_terms(place, plan, left_levels, right_levels, pieces, lefts, fits)
    far = [shift(far[0], 1), shift(far[1], fits - 1)]
    returned = to_orb(back)
    own, rise, fall = near_terms(place, amps, rows, fits)
    rise, fall = merge(rise, fall, far)
    below, above = shift(rise, 1), shift(fall, fits - 1)
    total = to_all(sum_returned(place, wanted, returned, orbs, fits, after=[rise]))
    return tuple(add_all(place, own, below, above, total, fits))


def solution(mesh):
    placed = (P("orb", None, "fit"), P(), P(), P(), P("orb", None))
    return jax.shard_map(
        on_device,
        mesh=mesh,
        in_specs=placed,
        out_specs=(P("orb", None, "fit"), P("orb", None, "fit")),
        check_vma=False,
    )
```

```python
import jax
import jax.numpy as jnp
from jax import lax
from jax.experimental import pallas as pl
from jax.experimental.pallas import tpu as pltpu
from jax.sharding import PartitionSpec as P

TILE = 128
SUB = 16
WIDE = 256
DIGITS = ((2, 1), (4, 2), (4, 8))
F32 = jnp.float32
BF16 = jnp.bfloat16
MIB = 1024 * 1024


ORB, FIT, BACK, MINE, NEXT = 0, 1, 2, 6, 10

SMEM = pl.BlockSpec(memory_space=pltpu.SMEM)
ANY = pl.BlockSpec(memory_space=pl.ANY)


def sds(shape, dtype):
    return jax.ShapeDtypeStruct(shape, dtype)


def whole(shape):
    return pl.BlockSpec(shape, lambda n: (0,) * len(shape))


def call(kernel, grid, in_specs, out_specs, out_shape, args, scratch=(), memory=56, aliases=None, name=None):
    return pl.pallas_call(
        kernel,
        grid=(grid,),
        in_specs=in_specs,
        out_specs=out_specs,
        out_shape=out_shape,
        scratch_shapes=list(scratch),
        compiler_params=pltpu.CompilerParams(vmem_limit_bytes=memory * MIB),
        cost_estimate=pl.CostEstimate(flops=0, bytes_accessed=1024, transcendentals=0),
        input_output_aliases=aliases or {},
        name=name,
    )(*args)


def device_of(m, fits, cols):
    return m // (fits * cols), m // cols % fits, m % cols


def list_row(me, d):
    return sum(((me // stride - d // stride) & (count - 1)) * stride for count, stride in DIGITS)


def pack_blocks(place, blocks, peers, fits):
    orbs, virt, aux = blocks.shape
    cols = aux // 128
    rows = TILE // fits
    steps = 4
    block = peers // steps

    def kernel(place_ref, blocks_ref, out_ref):
        @pl.loop(0, block)
        def _(n):
            m = pl.program_id(0) * block + n
            h, turned, c = m // (fits * cols), m // cols % fits, m % cols
            tile = place_ref[BACK + turned] * TILE
            lanes = pl.ds(pl.multiple_of(c * 128, 128), 128)
            for z in range(fits):
                at = pl.ds(pl.multiple_of(tile + z * rows + h * SUB, SUB), SUB)
                for k in range(orbs):
                    out_ref[n * fits + z, k] = blocks_ref[k, at, lanes]

    return call(
        kernel,
        steps,
        [SMEM, whole(blocks.shape)],
        pl.BlockSpec((block * fits, orbs, SUB, 128), lambda n: (n, 0, 0, 0)),
        sds((peers * fits, orbs, SUB, 128), BF16),
        (place, blocks),
        memory=16,
        name="pack_blocks",
    )


def pick_pieces(place, wanted, held, fits, after):
    peers, count = wanted.shape
    orbs = held.shape[1]
    held = held.reshape(-1, SUB, 128)
    block = peers // 4

    def kernel(place_ref, wanted_ref, held_ref, *refs):
        out_ref = refs[-1]
        parts = [place_ref[NEXT + s] * orbs for s in range(fits)]
        first = pl.program_id(0) * block

        @pl.loop(0, block)
        def _(d):
            row = list_row(place_ref[ORB], first + d)
            for g in range(count):
                spot = wanted_ref[row, g]
                for s in range(fits):
                    out_ref[d, g * fits + s] = held_ref[spot + parts[s]]

    return call(
        kernel,
        4,
        [SMEM, SMEM, whole(held.shape)] + [ANY] * len(after),
        pl.BlockSpec((block, count * fits, SUB, 128), lambda n: (n, 0, 0, 0)),
        sds((peers, count * fits, SUB, 128), BF16),
        (place, wanted, held, *after),
        name="pick_pieces",
    )


def pair_terms(place, plan, left_levels, right_levels, pieces, lefts, fits):
    orbs, virt, aux = lefts[0][0].shape
    peers, count = pieces.shape[0], pieces.shape[1] // fits
    tiles, cols = virt // TILE, aux // 128
    rows = TILE // fits
    taken = tiles * rows
    wide = virt // fits
    half = orbs // 2
    steps = count // 2
    names = ("left", "nleft", "nright")

    def kernel(place_ref, left_ref, nleft_ref, nright_ref, low_ref, high_ref, pieces_ref, *refs):
        sources, refs = refs[: len(lefts)], refs[len(lefts) :]
        out_ref, all_out_ref, rows_out_ref, *far_refs = refs[:5]
        lefts_ref, rows_ref, turned_ref, amp_ref, all_ref, sems = refs[5:]
        n = pl.program_id(0)
        copies = [
            pltpu.make_async_copy(source, lefts_ref.at[s, first : first + array.shape[0]], sems.at[k])
            for k, (source, (array, s, first)) in enumerate(zip(sources, lefts))
        ]

        @pl.when(n == 0)
        def _():
            for copy in copies:
                copy.start()
            all_ref[...] = jnp.zeros_like(all_ref)

        def group(g, e):
            for m in range(peers):
                h, turned, c = device_of(m, fits, cols)
                for s in range(fits):
                    at = pl.multiple_of(place_ref[BACK + (turned - s) % fits] * rows + h * SUB, SUB)
                    rows_out_ref[e, pl.ds(at, SUB), s * aux + c * 128 : s * aux + (c + 1) * 128] = pieces_ref[m, e * fits + s]

            if e == 0:

                @pl.when(n == 0)
                def _():
                    for copy in copies:
                        copy.wait()

            rows_ref[g] = rows_out_ref[e]
            turned_ref[e] = rows_out_ref[e].T
            row_id = lax.broadcasted_iota(jnp.int32, (WIDE, taken), 0)
            col_id = lax.broadcasted_iota(jnp.int32, (WIDE, taken), 1)
            for u in range(2):
                p = 2 * g + u
                k = left_ref[p]
                for start in range(0, virt, WIDE):
                    at = slice(start, start + WIDE)
                    total = jnp.zeros((WIDE, taken), F32)
                    for s in range(fits):
                        total += (
                            jnp.dot(
                                lefts_ref[s, k, at, :],
                                turned_ref[e, s * aux : (s + 1) * aux, :],
                                preferred_element_type=F32,
                            )
                            .astype(BF16)
                            .astype(F32)
                        )
                    keep = (row_id < nleft_ref[p] * TILE - start) & (col_id < nright_ref[g] * rows)
                    amp = jnp.where(keep, -total / (low_ref[k, at, :] + high_ref[g]), 0.0).astype(BF16)
                    all_ref[k, at, pl.ds(pl.multiple_of(g * taken, taken), taken)] = amp
                    amp_ref[e, u, :, at] = amp.T
            k0, k1 = left_ref[2 * g], left_ref[2 * g + 1]
            for s in range(fits):
                for start in range(0, aux, WIDE):
                    lanes = slice(start, start + WIDE)
                    back = (
                        jnp.dot(amp_ref[e, 0], lefts_ref[s, k0, :, lanes], preferred_element_type=F32)
                        + jnp.dot(amp_ref[e, 1], lefts_ref[s, k1, :, lanes], preferred_element_type=F32)
                    ).astype(BF16)
                    for t in range(tiles):
                        turned = place_ref[NEXT + (s + t) % fits]
                        for h in range(rows // SUB):
                            for c in range(WIDE // 128):
                                out_ref[(h * fits + turned) * cols + start // 128 + c, e * tiles + t] = back[
                                    t * rows + h * SUB : t * rows + (h + 1) * SUB, c * 128 : (c + 1) * 128
                                ]

        @pl.when(n < steps)
        def _():
            for e in range(2):
                group(2 * n + e, e)

        for low in range(2):

            @pl.when((n >= steps + low * half) & (n < steps + (low + 1) * half))
            def _(low=low):
                k = n - steps
                all_out_ref[0] = all_ref[k]
                sum_part(place_ref, all_ref.at[k], rows_ref, fits // 2, far_refs[low])

    block = (1, virt, aux + wide)
    places = [
        pl.BlockSpec(block, lambda n: (jnp.clip(n - steps, 0, half - 1), 0, 0)),
        pl.BlockSpec(block, lambda n: (jnp.clip(n - steps - half, 0, half - 1), 0, 0)),
    ]
    return call(
        kernel,
        steps + orbs,
        [SMEM] * 4
        + [
            whole(left_levels.shape),
            whole(right_levels.shape),
            pl.BlockSpec((peers, 2 * fits, SUB, 128), lambda n: (0, jnp.minimum(n, steps - 1), 0, 0)),
        ]
        + [ANY] * len(lefts),
        [
            pl.BlockSpec((peers, 2 * tiles, SUB, 128), lambda n: (0, jnp.minimum(n, steps - 1), 0, 0)),
        ]
        + [
            pl.BlockSpec((1, virt, count * taken), lambda n: (jnp.maximum(n - steps, 0), 0, 0)),
            pl.BlockSpec((2, taken, fits * aux), lambda n: (jnp.minimum(n, steps - 1), 0, 0)),
        ]
        + places,
        [
            sds((peers, count * tiles, SUB, 128), BF16),
            sds((orbs, virt, count * taken), BF16),
            sds((count, taken, fits * aux), BF16),
        ]
        + [sds((half, virt, aux + wide), BF16)] * 2,
        (place, *[plan[n] for n in names], left_levels, right_levels, pieces, *[array for array, _, _ in lefts]),
        scratch=[
            pltpu.VMEM((fits, orbs, virt, aux), BF16),
            pltpu.VMEM((count, taken, fits * aux), BF16),
            pltpu.VMEM((2, fits * aux, taken), BF16),
            pltpu.VMEM((2, 2, taken, virt), BF16),
            pltpu.VMEM((orbs, virt, count * taken), BF16),
            pltpu.SemaphoreType.DMA((len(lefts),)),
        ],
        name="pair_terms",
    )


def sum_part(place_ref, all_ref, rows_ref, s, out_ref):
    virt, depth = all_ref.shape
    aux = out_ref.shape[2] * rows_ref.shape[2] // (rows_ref.shape[2] + virt)
    wide = out_ref.shape[2] - aux
    for start in range(0, aux, WIDE):
        right = rows_ref[:, :, s * aux + start : s * aux + start + WIDE].reshape(depth, WIDE)
        out_ref[0, :, start : start + WIDE] = jnp.dot(
            all_ref[...], right, preferred_element_type=F32
        ).astype(BF16)
    mine = pl.ds(pl.multiple_of(place_ref[NEXT + s] * wide, wide), wide)
    out_ref[0, :, aux : aux + wide] = lax.dot_general(
        all_ref[...], all_ref[mine, :], (((1,), (1,)), ((), ())), preferred_element_type=F32
    ).astype(BF16)


def near_terms(place, amps, rows, fits):
    orbs, virt, depth = amps.shape
    aux = rows.shape[2] // fits
    block = (1, virt, aux + virt // fits)

    def kernel(place_ref, all_ref, rows_ref, *out_refs):
        for s, out_ref in zip((0, 1, fits - 1), out_refs):
            sum_part(place_ref, all_ref.at[0], rows_ref, s, out_ref)

    return call(
        kernel,
        orbs,
        [SMEM, pl.BlockSpec((1, virt, depth), lambda k: (k, 0, 0)), whole(rows.shape)],
        [pl.BlockSpec(block, lambda k: (k, 0, 0))] * 3,
        [sds((orbs, *block[1:]), BF16)] * 3,
        (place, amps, rows),
        name="near_terms",
    )


def merge(rise, fall, far):
    orbs, virt, width = rise.shape
    half = orbs // 2

    def kernel(a_ref, b_ref, c_ref, d_ref, up_ref, down_ref):
        up_ref[...] = (a_ref[...].astype(F32) + c_ref[...].astype(F32)).astype(BF16)
        down_ref[...] = (b_ref[...].astype(F32) + d_ref[...].astype(F32)).astype(BF16)

    block = (1, virt, width)
    low = pl.BlockSpec(block, lambda n: (n, 0, 0))
    high = pl.BlockSpec(block, lambda n: (n + half, 0, 0))
    return call(
        kernel,
        half,
        [low, high, low, low],
        [low, high],
        [sds(rise.shape, BF16)] * 2,
        (rise, fall, *far),
        aliases={0: 0, 1: 1},
        memory=16,
        name="merge",
    )


def sum_returned(place, wanted, returned, orbs, fits, after):
    peers, count = wanted.shape
    tiles = fits
    steps = 4
    block = peers // steps

    def kernel(place_ref, wanted_ref, part_ref, *refs):
        out_ref, total_ref = refs[len(after) :]
        n = pl.program_id(0)

        @pl.when(n == 0)
        def _():
            total_ref[...] = jnp.zeros_like(total_ref)

        @pl.loop(0, block)
        def _(d):
            row = list_row(place_ref[ORB], n * block + d)
            for g in range(count):
                spot = wanted_ref[row, g]
                for t in range(tiles):
                    total_ref[spot + t * orbs] += part_ref[d, g * tiles + t].astype(F32)

        @pl.when(n == steps - 1)
        def _():
            tile = [place_ref[MINE + q] for q in range(fits)]

            @pl.loop(0, peers)
            def _(o):
                for q in range(fits):
                    out_ref[o * fits + q] = total_ref[pl.ds((o * tiles + tile[q]) * orbs, orbs)].astype(BF16)

    out = (peers * fits, orbs, SUB, 128)
    return call(
        kernel,
        steps,
        [SMEM, SMEM, pl.BlockSpec((block, count * tiles, SUB, 128), lambda n: (n, 0, 0, 0))] + [ANY] * len(after),
        whole(out),
        sds(out, BF16),
        (place, wanted, returned, *after),
        scratch=[pltpu.VMEM((peers * orbs * tiles, SUB, 128), F32)],
        name="sum_returned",
    )


def add_all(place, own, below, above, sums, fits):
    orbs, virt, width = own.shape
    wide = virt // fits
    aux = width - wide
    cols = aux // 128
    rows = TILE // fits
    peers = sums.shape[0] // fits

    def kernel(place_ref, own_ref, below_ref, above_ref, sums_ref, gamma_ref, dens_ref):
        total = own_ref[0].astype(F32) + below_ref[0].astype(F32) + above_ref[0].astype(F32)
        gamma_ref[0] = total[:, 0:aux]
        dens_ref[0] = total[:, aux:width]
        for m in range(peers):
            h, turned, c = device_of(m, fits, cols)
            tile = place_ref[BACK + turned] * TILE
            lanes = slice(c * 128, (c + 1) * 128)
            for z in range(fits):
                at = pl.ds(pl.multiple_of(tile + z * rows + h * SUB, SUB), SUB)
                gamma_ref[0, at, lanes] += sums_ref[m * fits + z, 0].astype(F32)

    block = pl.BlockSpec((1, virt, width), lambda k: (k, 0, 0))
    return call(
        kernel,
        orbs,
        [SMEM, block, block, block, pl.BlockSpec((peers * fits, 1, SUB, 128), lambda k: (0, k, 0, 0))],
        [pl.BlockSpec((1, virt, aux), lambda k: (k, 0, 0)), pl.BlockSpec((1, virt, wide), lambda k: (k, 0, 0))],
        [sds((orbs, virt, aux), F32), sds((orbs, virt, wide), F32)],
        (place, own, below, above, sums),
        name="add_all",
    )


def on_device(blocks, occ_energy, virt_energy, domains, pairs):
    peers = lax.axis_size("orb")
    fits = lax.axis_size("fit")
    orbs, virt, aux = blocks.shape
    cols = aux // 128
    orb, fit = lax.axis_index("orb"), lax.axis_index("fit")
    steps = jnp.arange(fits, dtype=jnp.int32)
    place = jnp.concatenate(
        [jnp.stack([orb, fit]), (steps - fit) % fits, (orb // cols - steps) % fits, (fit + steps) % fits]
    ).astype(jnp.int32)

    def shift(x, k):
        return lax.ppermute(x, "fit", [(n, (n + k) % fits) for n in range(fits)])

    def to_orb(x):
        return lax.all_to_all(x, "orb", split_axis=0, concat_axis=0, tiled=True)

    def to_all(x):
        return lax.all_to_all(x, ("orb", "fit"), split_axis=0, concat_axis=0, tiled=True)

    one = [blocks[k : k + 1] for k in range(orbs)]
    last0, next3 = shift(one[0], 1), shift(one[3], fits - 1)
    right = pairs[::2, 1]
    groups = right.shape[0]
    held = to_all(pack_blocks(place, blocks, peers, fits))
    wanted = jnp.pad((right // orbs * (fits * orbs) + right % orbs)[None], ((0, 0), (0, 128 - groups)))
    for count, stride in DIGITS:
        wanted = jnp.concatenate(
            [wanted]
            + [
                lax.ppermute(wanted, "orb", [(n, n + ((n // stride + k) % count - n // stride % count) * stride) for n in range(peers)])
                for k in range(1, count)
            ]
        )
    wanted = wanted[:, :groups]
    spans = domains // TILE
    plan = dict(
        left=pairs[:, 0] - orb.astype(jnp.int32) * orbs,
        nleft=jnp.take(spans, pairs[:, 0]),
        nright=jnp.take(spans, right),
    )
    local = orb.astype(jnp.int32) * orbs + jnp.arange(orbs, dtype=jnp.int32)
    left_levels = (jnp.take(virt_energy, local, axis=0) - jnp.take(occ_energy, local)[:, None])[:, :, None]
    right_levels = jnp.take(virt_energy, right, axis=0) - jnp.take(occ_energy, right)[:, None]
    right_levels = lax.dynamic_slice_in_dim(
        right_levels.reshape(groups, -1, TILE), fit * (TILE // fits), TILE // fits, axis=2
    ).reshape(groups, 1, virt // fits)

    pieces = to_orb(pick_pieces(place, wanted, held, fits, after=[last0, next3]))
    last, next_ = shift(blocks[1:], 1), shift(blocks[:-1], fits - 1)
    far0, far3 = shift(last0, 1), shift(next3, fits - 1)
    far1, far2 = shift(last[:1], 1), shift(next_[-1:], fits - 1)
    lefts = [(blocks, 0, 0), (next_, 1, 0), (next3, 1, orbs - 1), (last0, 3, 0), (last, 3, 1)]
    lefts += [(far0, 2, 0), (far1, 2, 1), (far2, 2, 2), (far3, 2, 3)]
    back, amps, rows, *far = pair_terms(place, plan, left_levels, right_levels, pieces, lefts, fits)
    far = [shift(far[0], 1), shift(far[1], fits - 1)]
    returned = to_orb(back)
    own, rise, fall = near_terms(place, amps, rows, fits)
    rise, fall = merge(rise, fall, far)
    below, above = shift(rise, 1), shift(fall, fits - 1)
    total = to_all(sum_returned(place, wanted, returned, orbs, fits, after=[rise]))
    return tuple(add_all(place, own, below, above, total, fits))


def solution(mesh):
    placed = (P("orb", None, "fit"), P(), P(), P(), P("orb", None))
    return jax.shard_map(
        on_device,
        mesh=mesh,
        in_specs=placed,
        out_specs=(P("orb", None, "fit"), P("orb", None, "fit")),
        check_vma=False,
    )
```

```python
import jax
import jax.numpy as jnp
from jax import lax
from jax.experimental import pallas as pl
from jax.experimental.pallas import tpu as pltpu
from jax.sharding import PartitionSpec as P

TILE = 128
SUB = 16
WIDE = 256
DIGITS = ((2, 1), (4, 2), (4, 8))
F32 = jnp.float32
BF16 = jnp.bfloat16
MIB = 1024 * 1024


ORB, FIT, BACK, MINE, NEXT = 0, 1, 2, 6, 10

SMEM = pl.BlockSpec(memory_space=pltpu.SMEM)
ANY = pl.BlockSpec(memory_space=pl.ANY)


def sds(shape, dtype):
    return jax.ShapeDtypeStruct(shape, dtype)


def whole(shape):
    return pl.BlockSpec(shape, lambda n: (0,) * len(shape))


def call(kernel, grid, in_specs, out_specs, out_shape, args, scratch=(), memory=56, aliases=None, name=None):
    return pl.pallas_call(
        kernel,
        grid=(grid,),
        in_specs=in_specs,
        out_specs=out_specs,
        out_shape=out_shape,
        scratch_shapes=list(scratch),
        compiler_params=pltpu.CompilerParams(vmem_limit_bytes=memory * MIB),
        cost_estimate=pl.CostEstimate(flops=0, bytes_accessed=1024, transcendentals=0),
        input_output_aliases=aliases or {},
        name=name,
    )(*args)


def device_of(m, fits, cols):
    return m // (fits * cols), m // cols % fits, m % cols


def list_row(me, d):
    return sum(((me // stride - d // stride) & (count - 1)) * stride for count, stride in DIGITS)


def pack_blocks(place, blocks, peers, fits):
    orbs, virt, aux = blocks.shape
    cols = aux // 128
    rows = TILE // fits
    steps = 4
    block = peers // steps

    def kernel(place_ref, blocks_ref, out_ref):
        @pl.loop(0, block)
        def _(n):
            m = pl.program_id(0) * block + n
            h, turned, c = m // (fits * cols), m // cols % fits, m % cols
            tile = place_ref[BACK + turned] * TILE
            lanes = pl.ds(pl.multiple_of(c * 128, 128), 128)
            for z in range(fits):
                at = pl.ds(pl.multiple_of(tile + z * rows + h * SUB, SUB), SUB)
                for k in range(orbs):
                    out_ref[n * fits + z, k] = blocks_ref[k, at, lanes]

    return call(
        kernel,
        steps,
        [SMEM, whole(blocks.shape)],
        pl.BlockSpec((block * fits, orbs, SUB, 128), lambda n: (n, 0, 0, 0)),
        sds((peers * fits, orbs, SUB, 128), BF16),
        (place, blocks),
        memory=16,
        name="pack_blocks",
    )


def pick_pieces(place, wanted, held, fits, after):
    peers, count = wanted.shape
    orbs = held.shape[1]
    held = held.reshape(-1, SUB, 128)
    block = peers // 4

    def kernel(place_ref, wanted_ref, held_ref, *refs):
        out_ref = refs[-1]
        parts = [place_ref[NEXT + s] * orbs for s in range(fits)]
        first = pl.program_id(0) * block

        @pl.loop(0, block)
        def _(d):
            row = list_row(place_ref[ORB], first + d)
            for g in range(count):
                spot = wanted_ref[row, g]
                for s in range(fits):
                    out_ref[d, g * fits + s] = held_ref[spot + parts[s]]

    return call(
        kernel,
        4,
        [SMEM, SMEM, whole(held.shape)] + [ANY] * len(after),
        pl.BlockSpec((block, count * fits, SUB, 128), lambda n: (n, 0, 0, 0)),
        sds((peers, count * fits, SUB, 128), BF16),
        (place, wanted, held, *after),
        name="pick_pieces",
    )


def pair_terms(place, plan, left_levels, right_levels, pieces, lefts, fits):
    orbs, virt, aux = lefts[0][0].shape
    peers, count = pieces.shape[0], pieces.shape[1] // fits
    tiles, cols = virt // TILE, aux // 128
    rows = TILE // fits
    taken = tiles * rows
    wide = virt // fits
    half = orbs // 2
    steps = count // 2
    names = ("left", "nleft", "nright")

    def kernel(place_ref, left_ref, nleft_ref, nright_ref, low_ref, high_ref, pieces_ref, *refs):
        sources, refs = refs[: len(lefts)], refs[len(lefts) :]
        out_ref, all_out_ref, rows_out_ref, *far_refs = refs[:5]
        lefts_ref, rows_ref, turned_ref, amp_ref, all_ref, sems = refs[5:]
        n = pl.program_id(0)
        copies = [
            pltpu.make_async_copy(source, lefts_ref.at[s, first : first + array.shape[0]], sems.at[k])
            for k, (source, (array, s, first)) in enumerate(zip(sources, lefts))
        ]

        @pl.when(n == 0)
        def _():
            for copy in copies:
                copy.start()
            all_ref[...] = jnp.zeros_like(all_ref)

        def group(g, e):
            for m in range(peers):
                h, turned, c = device_of(m, fits, cols)
                for s in range(fits):
                    at = pl.multiple_of(place_ref[BACK + (turned - s) % fits] * rows + h * SUB, SUB)
                    rows_out_ref[e, pl.ds(at, SUB), s * aux + c * 128 : s * aux + (c + 1) * 128] = pieces_ref[m, e * fits + s]

            if e == 0:

                @pl.when(n == 0)
                def _():
                    for copy in copies:
                        copy.wait()

            rows_ref[g] = rows_out_ref[e]
            turned_ref[e] = rows_out_ref[e].T
            row_id = lax.broadcasted_iota(jnp.int32, (WIDE, taken), 0)
            col_id = lax.broadcasted_iota(jnp.int32, (WIDE, taken), 1)
            for u in range(2):
                p = 2 * g + u
                k = left_ref[p]
                for start in range(0, virt, WIDE):
                    at = slice(start, start + WIDE)
                    total = jnp.zeros((WIDE, taken), F32)
                    for s in range(fits):
                        total += (
                            jnp.dot(
                                lefts_ref[s, k, at, :],
                                turned_ref[e, s * aux : (s + 1) * aux, :],
                                preferred_element_type=F32,
                            )
                            .astype(BF16)
                            .astype(F32)
                        )
                    keep = (row_id < nleft_ref[p] * TILE - start) & (col_id < nright_ref[g] * rows)
                    amp = jnp.where(keep, -total / (low_ref[k, at, :] + high_ref[g]), 0.0).astype(BF16)
                    all_ref[k, at, pl.ds(pl.multiple_of(g * taken, taken), taken)] = amp
                    amp_ref[e, u, :, at] = amp.T
            k0, k1 = left_ref[2 * g], left_ref[2 * g + 1]
            for s in range(fits):
                for start in range(0, aux, WIDE):
                    lanes = slice(start, start + WIDE)
                    back = (
                        jnp.dot(amp_ref[e, 0], lefts_ref[s, k0, :, lanes], preferred_element_type=F32)
                        + jnp.dot(amp_ref[e, 1], lefts_ref[s, k1, :, lanes], preferred_element_type=F32)
                    ).astype(BF16)
                    for t in range(tiles):
                        turned = place_ref[NEXT + (s + t) % fits]
                        for h in range(rows // SUB):
                            for c in range(WIDE // 128):
                                out_ref[(h * fits + turned) * cols + start // 128 + c, e * tiles + t] = back[
                                    t * rows + h * SUB : t * rows + (h + 1) * SUB, c * 128 : (c + 1) * 128
                                ]

        @pl.when(n < steps)
        def _():
            for e in range(2):
                group(2 * n + e, e)

        for low in range(2):

            @pl.when((n >= steps + low * half) & (n < steps + (low + 1) * half))
            def _(low=low):
                k = n - steps
                all_out_ref[0] = all_ref[k]
                sum_part(place_ref, all_ref.at[k], rows_ref, fits // 2, far_refs[low])

    block = (1, virt, aux + wide)
    places = [
        pl.BlockSpec(block, lambda n: (jnp.clip(n - steps, 0, half - 1), 0, 0)),
        pl.BlockSpec(block, lambda n: (jnp.clip(n - steps - half, 0, half - 1), 0, 0)),
    ]
    return call(
        kernel,
        steps + orbs,
        [SMEM] * 4
        + [
            whole(left_levels.shape),
            whole(right_levels.shape),
            pl.BlockSpec((peers, 2 * fits, SUB, 128), lambda n: (0, jnp.minimum(n, steps - 1), 0, 0)),
        ]
        + [ANY] * len(lefts),
        [
            pl.BlockSpec((peers, 2 * tiles, SUB, 128), lambda n: (0, jnp.minimum(n, steps - 1), 0, 0)),
        ]
        + [
            pl.BlockSpec((1, virt, count * taken), lambda n: (jnp.maximum(n - steps, 0), 0, 0)),
            pl.BlockSpec((2, taken, fits * aux), lambda n: (jnp.minimum(n, steps - 1), 0, 0)),
        ]
        + places,
        [
            sds((peers, count * tiles, SUB, 128), BF16),
            sds((orbs, virt, count * taken), BF16),
            sds((count, taken, fits * aux), BF16),
        ]
        + [sds((half, virt, aux + wide), BF16)] * 2,
        (place, *[plan[n] for n in names], left_levels, right_levels, pieces, *[array for array, _, _ in lefts]),
        scratch=[
            pltpu.VMEM((fits, orbs, virt, aux), BF16),
            pltpu.VMEM((count, taken, fits * aux), BF16),
            pltpu.VMEM((2, fits * aux, taken), BF16),
            pltpu.VMEM((2, 2, taken, virt), BF16),
            pltpu.VMEM((orbs, virt, count * taken), BF16),
            pltpu.SemaphoreType.DMA((len(lefts),)),
        ],
        name="pair_terms",
    )


def sum_part(place_ref, all_ref, rows_ref, s, out_ref):
    virt, depth = all_ref.shape
    aux = out_ref.shape[2] * rows_ref.shape[2] // (rows_ref.shape[2] + virt)
    wide = out_ref.shape[2] - aux
    for start in range(0, aux, WIDE):
        right = rows_ref[:, :, s * aux + start : s * aux + start + WIDE].reshape(depth, WIDE)
        out_ref[0, :, start : start + WIDE] = jnp.dot(
            all_ref[...], right, preferred_element_type=F32
        ).astype(BF16)
    mine = pl.ds(pl.multiple_of(place_ref[NEXT + s] * wide, wide), wide)
    out_ref[0, :, aux : aux + wide] = lax.dot_general(
        all_ref[...], all_ref[mine, :], (((1,), (1,)), ((), ())), preferred_element_type=F32
    ).astype(BF16)


def near_terms(place, amps, rows, fits):
    orbs, virt, depth = amps.shape
    aux = rows.shape[2] // fits
    block = (1, virt, aux + virt // fits)

    def kernel(place_ref, all_ref, rows_ref, *out_refs):
        for s, out_ref in zip((0, 1, fits - 1), out_refs):
            sum_part(place_ref, all_ref.at[0], rows_ref, s, out_ref)

    return call(
        kernel,
        orbs,
        [SMEM, pl.BlockSpec((1, virt, depth), lambda k: (k, 0, 0)), whole(rows.shape)],
        [pl.BlockSpec(block, lambda k: (k, 0, 0))] * 3,
        [sds((orbs, *block[1:]), BF16)] * 3,
        (place, amps, rows),
        name="near_terms",
    )


def merge(rise, fall, far):
    orbs, virt, width = rise.shape
    half = orbs // 2

    def kernel(a_ref, b_ref, c_ref, d_ref, up_ref, down_ref):
        up_ref[...] = (a_ref[...].astype(F32) + c_ref[...].astype(F32)).astype(BF16)
        down_ref[...] = (b_ref[...].astype(F32) + d_ref[...].astype(F32)).astype(BF16)

    block = (1, virt, width)
    low = pl.BlockSpec(block, lambda n: (n, 0, 0))
    high = pl.BlockSpec(block, lambda n: (n + half, 0, 0))
    return call(
        kernel,
        half,
        [low, high, low, low],
        [low, high],
        [sds(rise.shape, BF16)] * 2,
        (rise, fall, *far),
        aliases={0: 0, 1: 1},
        memory=16,
        name="merge",
    )


def sum_returned(place, wanted, returned, orbs, fits, after):
    peers, count = wanted.shape
    tiles = fits
    steps = 4
    block = peers // steps

    def kernel(place_ref, wanted_ref, part_ref, *refs):
        out_ref, total_ref = refs[len(after) :]
        n = pl.program_id(0)

        @pl.when(n == 0)
        def _():
            total_ref[...] = jnp.zeros_like(total_ref)

        @pl.loop(0, block)
        def _(d):
            row = list_row(place_ref[ORB], n * block + d)
            for g in range(count):
                spot = wanted_ref[row, g]
                for t in range(tiles):
                    total_ref[spot + t * orbs] += part_ref[d, g * tiles + t].astype(F32)

        @pl.when(n == steps - 1)
        def _():
            tile = [place_ref[MINE + q] for q in range(fits)]

            @pl.loop(0, peers)
            def _(o):
                for q in range(fits):
                    out_ref[o * fits + q] = total_ref[pl.ds((o * tiles + tile[q]) * orbs, orbs)].astype(BF16)

    out = (peers * fits, orbs, SUB, 128)
    return call(
        kernel,
        steps,
        [SMEM, SMEM, pl.BlockSpec((block, count * tiles, SUB, 128), lambda n: (n, 0, 0, 0))] + [ANY] * len(after),
        whole(out),
        sds(out, BF16),
        (place, wanted, returned, *after),
        scratch=[pltpu.VMEM((peers * orbs * tiles, SUB, 128), F32)],
        name="sum_returned",
    )


def add_all(place, own, below, above, sums, fits):
    orbs, virt, width = own.shape
    wide = virt // fits
    aux = width - wide
    cols = aux // 128
    rows = TILE // fits
    peers = sums.shape[0] // fits

    def kernel(place_ref, own_ref, below_ref, above_ref, sums_ref, gamma_ref, dens_ref):
        total = own_ref[0].astype(F32) + below_ref[0].astype(F32) + above_ref[0].astype(F32)
        gamma_ref[0] = total[:, 0:aux]
        dens_ref[0] = total[:, aux:width]
        for m in range(peers):
            h, turned, c = device_of(m, fits, cols)
            tile = place_ref[BACK + turned] * TILE
            lanes = slice(c * 128, (c + 1) * 128)
            for z in range(fits):
                at = pl.ds(pl.multiple_of(tile + z * rows + h * SUB, SUB), SUB)
                gamma_ref[0, at, lanes] += sums_ref[m * fits + z, 0].astype(F32)

    block = pl.BlockSpec((1, virt, width), lambda k: (k, 0, 0))
    return call(
        kernel,
        orbs,
        [SMEM, block, block, block, pl.BlockSpec((peers * fits, 1, SUB, 128), lambda k: (0, k, 0, 0))],
        [pl.BlockSpec((1, virt, aux), lambda k: (k, 0, 0)), pl.BlockSpec((1, virt, wide), lambda k: (k, 0, 0))],
        [sds((orbs, virt, aux), F32), sds((orbs, virt, wide), F32)],
        (place, own, below, above, sums),
        name="add_all",
    )


def on_device(blocks, occ_energy, virt_energy, domains, pairs):
    peers = lax.axis_size("orb")
    fits = lax.axis_size("fit")
    orbs, virt, aux = blocks.shape
    cols = aux // 128
    orb, fit = lax.axis_index("orb"), lax.axis_index("fit")
    steps = jnp.arange(fits, dtype=jnp.int32)
    place = jnp.concatenate(
        [jnp.stack([orb, fit]), (steps - fit) % fits, (orb // cols - steps) % fits, (fit + steps) % fits]
    ).astype(jnp.int32)

    def shift(x, k):
        return lax.ppermute(x, "fit", [(n, (n + k) % fits) for n in range(fits)])

    def to_orb(x):
        return lax.all_to_all(x, "orb", split_axis=0, concat_axis=0, tiled=True)

    def to_all(x):
        return lax.all_to_all(x, ("orb", "fit"), split_axis=0, concat_axis=0, tiled=True)

    one = [blocks[k : k + 1] for k in range(orbs)]
    last0, next3 = shift(one[0], 1), shift(one[3], fits - 1)
    right = pairs[::2, 1]
    groups = right.shape[0]
    held = to_all(pack_blocks(place, blocks, peers, fits))
    wanted = jnp.pad((right // orbs * (fits * orbs) + right % orbs)[None], ((0, 0), (0, 128 - groups)))
    for count, stride in DIGITS:
        wanted = jnp.concatenate(
            [wanted]
            + [
                lax.ppermute(wanted, "orb", [(n, n + ((n // stride + k) % count - n // stride % count) * stride) for n in range(peers)])
                for k in range(1, count)
            ]
        )
    wanted = wanted[:, :groups]
    spans = domains // TILE
    plan = dict(
        left=pairs[:, 0] - orb.astype(jnp.int32) * orbs,
        nleft=jnp.take(spans, pairs[:, 0]),
        nright=jnp.take(spans, right),
    )
    local = orb.astype(jnp.int32) * orbs + jnp.arange(orbs, dtype=jnp.int32)
    left_levels = (jnp.take(virt_energy, local, axis=0) - jnp.take(occ_energy, local)[:, None])[:, :, None]
    right_levels = jnp.take(virt_energy, right, axis=0) - jnp.take(occ_energy, right)[:, None]
    right_levels = lax.dynamic_slice_in_dim(
        right_levels.reshape(groups, -1, TILE), fit * (TILE // fits), TILE // fits, axis=2
    ).reshape(groups, 1, virt // fits)

    pieces = to_orb(pick_pieces(place, wanted, held, fits, after=[last0, next3]))
    last1, next2 = shift(one[1], 1), shift(one[2], fits - 1)
    last2, next0 = shift(blocks[2:], 1), shift(blocks[:2], fits - 1)
    far0, far3 = shift(last0, 1), shift(next3, fits - 1)
    far1, far2 = shift(last1, 1), shift(next2, fits - 1)
    lefts = [(blocks, 0, 0), (next0, 1, 0), (next2, 1, 2), (next3, 1, 3)]
    lefts += [(last0, 3, 0), (last1, 3, 1), (last2, 3, 2)]
    lefts += [(far0, 2, 0), (far1, 2, 1), (far2, 2, 2), (far3, 2, 3)]
    back, amps, rows, *far = pair_terms(place, plan, left_levels, right_levels, pieces, lefts, fits)
    far = [shift(far[0], 1), shift(far[1], fits - 1)]
    returned = to_orb(back)
    own, rise, fall = near_terms(place, amps, rows, fits)
    rise, fall = merge(rise, fall, far)
    below, above = shift(rise, 1), shift(fall, fits - 1)
    total = to_all(sum_returned(place, wanted, returned, orbs, fits, after=[rise]))
    return tuple(add_all(place, own, below, above, total, fits))


def solution(mesh):
    placed = (P("orb", None, "fit"), P(), P(), P(), P("orb", None))
    return jax.shard_map(
        on_device,
        mesh=mesh,
        in_specs=placed,
        out_specs=(P("orb", None, "fit"), P("orb", None, "fit")),
        check_vma=False,
    )
```
